256 devices in a mesh: ga: 16 (over z, x_lo), ba: 16 (over y, x_hi, core).
Axes of the slice: x: 4 (x_hi: 2, x_lo: 2; x = x_hi * 2 + x_lo), y: 4, z: 8, core: 2. Of those that a mesh axis runs over, the one named last changes fastest.
Arguments:
- matrix_elements: bfloat16 [256, 64, 8192], P('ba', None, 'ga'), may hold values from -0.0625 to 0.0625
- screening: bfloat16 [8192, 8192], P(None, 'ga'), may hold values from -1 to 2
- band_factor: float32 [2, 256], P(None, 'ba'), may hold values from 0.5 to 5
- pair_list: int32 [2, 2016], replicated, may hold values from 0 to 63, as said below
Outputs:
- sigma: float32 [2, 2016], P(None, 'ga')
The draws below stay inside these ranges and needn't reach their ends.
Inputs may be any that keep to these rules, and one draw needn't show every extreme that they name: `pair_list`: each column is a pair (m, n) with m < n; every such pair of the 64 bands appears exactly once.
All inputs are finite; a program needn't handle non-finite values.
Results may differ from the reference program's by a relative error of at most 0.0003.
Values may be sent and summed in bfloat16 or wider, within the bound.
A program may use at most 128 MiB of HBM per device.

```python
import math
import jax
import jax.numpy as jnp
import numpy as np
from jax import lax

QP = 64
NFREQ = 2
NG = 8192
NV = 256
NPAIR = 2016


def draw_screening(key, part):
    key = jax.random.fold_in(key, 7)
    diag_key, off_key = jax.random.split(key)
    row_ids = lax.broadcasted_iota(jnp.int32, (NG, NG), 0)
    col_ids = lax.broadcasted_iota(jnp.int32, (NG, NG), 1)
    diagonal = jax.random.uniform(diag_key, (NG, NG), jnp.float32, 0.5, 2.0)
    off_diag = jax.random.normal(off_key, (NG, NG), jnp.float32) * (0.7 / math.sqrt(NG))
    off_diag = jnp.clip(off_diag, -1.0, 1.0)
    return jnp.where(row_ids == col_ids, diagonal, off_diag).astype(jnp.bfloat16)


def draw_pair_list(key, part):
    key = jax.random.fold_in(key, 11)
    upper = np.triu_indices(QP, 1)
    first_band = jnp.asarray(upper[0].astype(np.int32))
    second_band = jnp.asarray(upper[1].astype(np.int32))
    ordering = jax.random.permutation(key, NPAIR)
    return jnp.stack([first_band[ordering], second_band[ordering]]).astype(jnp.int32)


def block_levels(own_key, extent, shards, smallest, top_value):
    def one(dim, parts):
        heights = jax.random.uniform(jax.random.fold_in(jax.random.fold_in(own_key, 6), dim), (parts,), jnp.float32, smallest / len(shards), top_value / len(shards))
        return jnp.repeat(jnp.exp(heights), extent[dim] // parts).reshape((-1,) + (1,) * (len(extent) - dim - 1))

    loudness = one(*shards[0])
    for cut in shards[1:]:
        loudness = loudness * one(*cut)
    return loudness


def gaussian(rng, dims, width, limit, pieces=(), held_as=jnp.bfloat16):
    array = width * jax.random.normal(rng, dims, jnp.float32)
    if pieces:
        array = array * block_levels(rng, dims, pieces, -0.22, 0.18)
    return jnp.clip(array, -limit, limit).astype(held_as)


def setup_inputs(seed: int = 0) -> dict:
    key_of = jax.random.split(jax.random.key(seed), 5)
    matrix_elements = gaussian(key_of[0], (NV, QP, NG), NG ** -0.5, 0.0625, ((0, 16), (2, 16)))
    screening = draw_screening(jax.random.fold_in(key_of[4], 71), 0)
    band_factor = jnp.clip(jnp.exp(math.log(5.0) - 2.3025851 * jax.random.uniform(key_of[2], (NFREQ, NV), jnp.float32) ** block_levels(key_of[2], (NFREQ, NV), ((1, 16),), -0.2, 0.2)), 0.5, 5.0)
    pair_list = draw_pair_list(jax.random.fold_in(key_of[4], 71), 0)
    return {"matrix_elements": matrix_elements, "screening": screening, "band_factor": band_factor, "pair_list": pair_list}


def reference(matrix_elements, screening, band_factor, pair_list):
    def band_term(elements):
        applied_left = jnp.dot(elements, screening, preferred_element_type=jnp.float32)
        return jnp.dot(applied_left, elements.astype(jnp.float32).T, precision=lax.Precision.HIGHEST)

    per_band = lax.map(band_term, matrix_elements)
    full = jnp.einsum("fv,vmn->fmn", band_factor.astype(jnp.float32), per_band, precision=lax.Precision.HIGHEST)
    flattened = full.reshape(full.shape[0], QP * QP)
    flat_index = (pair_list[0] * QP + pair_list[1]).astype(jnp.int32)
    return jnp.take(flattened, flat_index, axis=1)
```

```python
import functools

import jax
import jax.numpy as jnp
from jax import lax
from jax.experimental import pallas as pl
from jax.experimental.pallas import tpu as pltpu
from jax.sharding import PartitionSpec as P

MESH = pl.DeviceIdType.MESH
GB = 512
CH = 256
NCH = 4
NBLK = 10
A0, A1, AM1, A2, AM2, B2 = range(6)
UP1, UP2, DN1, DN2, XF = range(5)
FOREIGN = (
    (A1, ((AM2, 0), (B2, 1))),
    (AM1, ((A2, 2), (B2, 3))),
    (AM2, ((A2, 4), (B2, 5))),
    (B2, ((A2, 6), (A1, 7), (A0, 8), (AM1, 9))),
)


def remote(src, dst, send, recv, device):
    return pltpu.make_async_remote_copy(
        src_ref=src, dst_ref=dst, send_sem=send, recv_sem=recv, device_id=device, device_id_type=MESH
    )


def wait_bytes(ref, sem):
    pltpu.make_async_copy(ref, ref, sem).wait()


def kernel(
    m_ref, w_ref, bf_ref, pair_ref, out_ref,
    mv, wown, wf, pp, one_n, facc, red_src, red_a, red_b,
    msend, mrecv, mloc, wloc, w1s, w1r, w2s, w2r, w3s, w3r, r1s, r1r, r2s, r2r,
):
    ga, ba = lax.axis_index("ga"), lax.axis_index("ba")
    z, s = ga // 2, lax.rem(ga, 2)
    y, xh, c = ba // 4, lax.rem(ba // 2, 2), lax.rem(ba, 2)

    def gai(dz, flip=0):
        side = 1 - s if flip else s
        return lax.rem(z + 8 + dz, 8) * 2 + side

    def bai(dy, dx, core):
        return (lax.rem(y + 4 + dy, 4) * 2 + lax.rem(xh + dx, 2)) * 2 + core

    barrier = pltpu.get_barrier_semaphore()

    @pl.loop(1, 16)
    def _(k):
        pl.semaphore_signal(barrier, inc=1, device_id=(lax.rem(ga + k, 16), ba), device_id_type=MESH)
        pl.semaphore_signal(barrier, inc=1, device_id=(ga, lax.rem(ba + k, 16)), device_id_type=MESH)

    own_m = pltpu.make_async_copy(m_ref, mv.at[A0], mloc)
    own_m.start()
    own_rows = ((A0, gai(0)), (A1, gai(1)), (AM1, gai(-1)), (A2, gai(2)), (AM2, gai(-2)), (B2, gai(2, 1)))
    own_w = []
    for slot, block in own_rows:
        cp = pltpu.make_async_copy(w_ref.at[pl.ds(block * GB, GB)], wown.at[slot], wloc.at[slot])
        cp.start()
        own_w.append(cp)

    pl.semaphore_wait(barrier, 30)

    w1 = []
    plan = (
        (gai(-1), ((gai(-3), 0), (gai(1, 1), 1))),
        (gai(1), ((gai(3), 2), (gai(3, 1), 3))),
        (gai(2), ((gai(4), 4), (gai(4, 1), 5))),
        (gai(-2, 1), ((gai(0, 1), 6), (gai(-1, 1), 7), (gai(-2, 1), 8), (gai(-3, 1), 9))),
    )
    for target, blocks in plan:
        for block, index in blocks:
            cp = remote(
                w_ref.at[pl.ds(block * GB + ba * 32, 32)], wf.at[ba, index], w1s, w1r, (target, ba)
            )
            cp.start()

    def hop(flow, k):
        rows = pl.ds(pl.multiple_of(k * CH, CH), CH)
        src, dst, target = {
            UP1: (m_ref, AM1, gai(1)),
            DN1: (m_ref, A1, gai(-1)),
            UP2: (mv.at[AM1], AM2, gai(1)),
            DN2: (mv.at[A1], A2, gai(-1)),
            XF: (mv.at[A2], B2, gai(0, 1)),
        }[flow]
        return remote(
            src.at[rows], mv.at[dst, rows], msend.at[flow, k], mrecv.at[flow, k], (target, ba)
        )

    @pl.loop(0, NCH)
    def _(k):
        hop(UP1, k).start()
        hop(DN1, k).start()

    pp[...] = jnp.full(pp.shape, -1, jnp.int32)
    for a in range(16):
        pp[:, a * 128 : a * 128 + 126] = pair_ref[:, a * 126 : (a + 1) * 126]
    band = lax.rem(lax.broadcasted_iota(jnp.int32, (256, 2048), 0), 64)
    one_n[...] = jnp.where(band == pp[1:2, :], 1.0, 0.0).astype(jnp.bfloat16)
    facc[...] = jnp.zeros_like(facc)

    wait_bytes(wf.at[ba], w1r)
    peers = [(q // 2, q % 2) for q in range(1, 8)]
    w2 = []
    for q, (dy, dx) in enumerate(peers):
        cp = remote(wf.at[ba], wf.at[ba], w2s.at[q], w2r.at[q], (ga, bai(dy, dx, c)))
        cp.start()
        w2.append(cp)
    cross = [remote(wf.at[ba], wf.at[ba], w3s.at[7], w3r.at[7], (ga, bai(0, 0, 1 - c)))]
    cross[0].start()

    @pl.loop(0, NCH)
    def _(k):
        hop(UP1, k).wait_recv()
        hop(UP2, k).start()
        hop(DN1, k).wait_recv()
        hop(DN2, k).start()

    for q, (dy, dx) in enumerate(peers):
        origin = bai(-dy, dx, c)
        w2[q].wait_recv()
        cp = remote(wf.at[origin], wf.at[origin], w3s.at[q], w3r.at[q], (ga, bai(0, 0, 1 - c)))
        cp.start()
        cross.append(cp)
    own_m.wait()
    for cp in own_w:
        cp.wait()
    for cp in cross:
        cp.wait_recv()

    lane = lax.broadcasted_iota(jnp.int32, (64, 256), 1) // 64

    def compute(k):
        rows = pl.ds(pl.multiple_of(k * CH, CH), CH)

        def second(col, applied):
            high = applied.astype(jnp.bfloat16)
            low = (applied - high.astype(jnp.float32)).astype(jnp.bfloat16)
            right = mv[col, rows, :]
            dims = (((1,), (1,)), ((), ()))
            return lax.dot_general(
                high, right, dims, preferred_element_type=jnp.float32
            ) + lax.dot_general(low, right, dims, preferred_element_type=jnp.float32)

        applied = jnp.zeros((CH, GB), jnp.float32)
        for slot in (A0, A1, AM1, A2, AM2, B2):
            applied += jnp.dot(mv[slot, rows, :], wown[slot], preferred_element_type=jnp.float32)
        per_band = second(A0, applied)
        for col, terms in FOREIGN:
            applied = jnp.zeros((CH, GB), jnp.float32)
            for slot, index in terms:
                block = wf[:, index].reshape(GB, GB)
                applied += jnp.dot(mv[slot, rows, :], block, preferred_element_type=jnp.float32)
            per_band += second(col, applied)
        for f in range(2):
            total = facc[pl.ds(f * 64, 64), :]
            for q in range(4):
                part = per_band[q * 64 : (q + 1) * 64, :]
                total += jnp.where(lane == q, part * bf_ref[f, k * 4 + q], 0.0)
            facc[pl.ds(f * 64, 64), :] = total

    @pl.loop(0, NCH + 1)
    def _(k):
        @pl.when(k < NCH)
        def _():
            hop(DN2, k).wait_recv()
            hop(XF, k).start()

        @pl.when(k >= 1)
        def _():
            hop(UP2, k - 1).wait_recv()
            hop(XF, k - 1).wait_recv()
            compute(k - 1)

    full = facc[...]
    x1 = full.astype(jnp.bfloat16)
    rest = full - x1.astype(jnp.float32)
    x2 = rest.astype(jnp.bfloat16)
    x3 = (rest - x2.astype(jnp.float32)).astype(jnp.bfloat16)
    picked = (
        jnp.dot(x1, one_n[...], preferred_element_type=jnp.float32)
        + jnp.dot(x2, one_n[...], preferred_element_type=jnp.float32)
        + jnp.dot(x3, one_n[...], preferred_element_type=jnp.float32)
    )
    first = lax.broadcasted_iota(jnp.int32, (64, 2048), 0) == pp[0:1, :]
    for f in range(2):
        row = jnp.sum(jnp.where(first, picked[f * 64 : (f + 1) * 64], 0.0), axis=0, keepdims=True)
        for a in range(16):
            red_src[a, f : f + 1, :] = row[:, a * 128 : (a + 1) * 128]

    @pl.loop(1, 16)
    def _(k):
        peer = lax.rem(ga + k, 16)
        remote(red_src.at[peer], red_a.at[k - 1], r1s, r1r, (peer, ba)).start()

    wait_bytes(red_a, r1r)
    mine = red_src[ga]
    for k in range(15):
        mine += red_a[k]
    red_b[ba] = mine

    @pl.loop(1, 16)
    def _(k):
        peer = lax.rem(ba + k, 16)
        remote(red_b.at[ba], red_b.at[ba], r2s, r2r, (ga, peer)).start()

    wait_bytes(red_b.at[pl.ds(0, 15)], r2r)
    total = red_b[0]
    for k in range(1, 16):
        total += red_b[k]
    out_ref[...] = total[:, :126]

    wait_bytes(wf.at[0], w1s)
    for cp in w2 + cross:
        cp.wait_send()

    @pl.loop(0, NCH)
    def _(k):
        for flow in (UP1, DN1, UP2, DN2, XF):
            hop(flow, k).wait_send()

    wait_bytes(red_a, r1s)
    wait_bytes(red_b.at[pl.ds(0, 15)], r2s)


def shards(matrix_elements, screening, band_factor, pair_list):
    bands, quasi, width = matrix_elements.shape
    dma = pltpu.SemaphoreType.DMA
    return pl.pallas_call(
        kernel,
        out_shape=jax.ShapeDtypeStruct((2, 126), jnp.float32),
        in_specs=[
            pl.BlockSpec(memory_space=pl.ANY),
            pl.BlockSpec(memory_space=pl.ANY),
            pl.BlockSpec(memory_space=pltpu.SMEM),
            pl.BlockSpec(memory_space=pltpu.VMEM),
        ],
        out_specs=pl.BlockSpec(memory_space=pltpu.VMEM),
        scratch_shapes=[
            pltpu.VMEM((6, 1024, GB), jnp.bfloat16),
            pltpu.VMEM((6, GB, GB), jnp.bfloat16),
            pltpu.VMEM((16, NBLK, 32, GB), jnp.bfloat16),
            pltpu.VMEM((2, 2048), jnp.int32),
            pltpu.VMEM((256, 2048), jnp.bfloat16),
            pltpu.VMEM((128, 256), jnp.float32),
            pltpu.VMEM((16, 2, 128), jnp.float32),
            pltpu.VMEM((15, 2, 128), jnp.float32),
            pltpu.VMEM((16, 2, 128), jnp.float32),
            dma((5, NCH)), dma((5, NCH)), dma, dma((6,)),
            dma, dma, dma((7,)), dma((7,)), dma((8,)), dma((8,)),
            dma, dma, dma, dma,
        ],
        compiler_params=pltpu.CompilerParams(
            collective_id=0, has_side_effects=True, vmem_limit_bytes=48 << 20
        ),
        cost_estimate=pl.CostEstimate(flops=9 * 10**9, bytes_accessed=20 << 20, transcendentals=0),
        name="self_energy",
    )(matrix_elements.reshape(bands * quasi, width), screening, band_factor, pair_list)


def solution(mesh):
    placed = (P("ba", None, "ga"), P(None, "ga"), P(None, "ba"), P())
    return jax.shard_map(
        shards, mesh=mesh, in_specs=placed, out_specs=P(None, "ga"), check_vma=False
    )
```

```python
import functools

import jax
import jax.numpy as jnp
from jax import lax
from jax.experimental import pallas as pl
from jax.experimental.pallas import tpu as pltpu
from jax.sharding import PartitionSpec as P

MESH = pl.DeviceIdType.MESH
GB = 512
CH = 128
NCH = 8
NBLK = 9
A0, A1, AM1, A2, AM2, B0, B2 = range(7)
UP1, UP2, DN1, DN2, X0, X2 = range(6)
NT = (((1,), (1,)), ((), ()))


def remote(src, dst, send, recv, device):
    return pltpu.make_async_remote_copy(
        src_ref=src, dst_ref=dst, send_sem=send, recv_sem=recv, device_id=device, device_id_type=MESH
    )


def wait_bytes(ref, sem):
    pltpu.make_async_copy(ref, ref, sem).wait()


def dot(a, b):
    return jnp.dot(a, b, preferred_element_type=jnp.float32)


def dot_nt(a, b):
    return lax.dot_general(a, b, NT, preferred_element_type=jnp.float32)


def halves(x):
    high = x.astype(jnp.bfloat16)
    return high, (x - high.astype(jnp.float32)).astype(jnp.bfloat16)


def kernel(
    m_ref, w_ref, bf_ref, pair_ref, out_ref,
    mv, wown, wf, t2, tm2, tb2, ab2, pairs, pp, one_n, facc, red_src, red_a, red_b,
    msend, mrecv, mloc, wloc, ploc, w1s, w1r, w2s, w2r, w3s, w3r, r1s, r1r, r2s, r2r,
):
    ga, ba = lax.axis_index("ga"), lax.axis_index("ba")
    z, s = ga // 2, lax.rem(ga, 2)
    y, xh, c = ba // 4, lax.rem(ba // 2, 2), lax.rem(ba, 2)

    def gai(dz, flip=0):
        side = 1 - s if flip else s
        return lax.rem(z + 8 + dz, 8) * 2 + side

    def bai(dy, dx, core):
        return (lax.rem(y + 4 + dy, 4) * 2 + lax.rem(xh + dx, 2)) * 2 + core

    def share(dy, dx, core):
        return (core * 4 + lax.rem(y + 4 + dy, 4)) * 2 + lax.rem(xh + dx, 2)

    barrier = pltpu.get_barrier_semaphore()

    @pl.loop(1, 16)
    def _(k):
        pl.semaphore_signal(barrier, inc=1, device_id=(lax.rem(ga + k, 16), ba), device_id_type=MESH)
        pl.semaphore_signal(barrier, inc=1, device_id=(ga, lax.rem(ba + k, 16)), device_id_type=MESH)

    own_p = pltpu.make_async_copy(pair_ref, pairs, ploc)
    own_p.start()
    own_m = pltpu.make_async_copy(m_ref, mv.at[A0], mloc)
    own_m.start()
    own_rows = (
        (A0, gai(0)), (A1, gai(1)), (AM1, gai(-1)), (A2, gai(2)), (AM2, gai(-2)),
        (B0, gai(0, 1)), (B2, gai(2, 1)),
    )
    own_w = []
    for slot, block in own_rows:
        cp = pltpu.make_async_copy(w_ref.at[pl.ds(block * GB, GB)], wown.at[slot], wloc.at[slot])
        cp.start()
        own_w.append(cp)

    pl.semaphore_wait(barrier, 30)

    mine_w = share(0, 0, c)
    plan = (
        (gai(2), ((gai(4), 6), (gai(4, 1), 7))),
        (gai(-2, 1), ((gai(-3, 1), 8),)),
        (gai(1), ((gai(3), 4), (gai(3, 1), 5))),
        (gai(-1), ((gai(-3), 3),)),
        (gai(0, 1), ((gai(-1, 1), 0), (gai(1, 1), 1), (gai(-2, 1), 2))),
    )
    for target, blocks in plan:
        for block, index in blocks:
            remote(
                w_ref.at[pl.ds(block * GB + mine_w * 32, 32)], wf.at[mine_w, index], w1s, w1r, (target, ba)
            ).start()

    def hop(flow, k):
        rows = pl.ds(pl.multiple_of(k * CH, CH), CH)
        src, dst, target = {
            UP1: (m_ref, AM1, gai(1)),
            DN1: (m_ref, A1, gai(-1)),
            UP2: (mv.at[AM1], AM2, gai(1)),
            DN2: (mv.at[A1], A2, gai(-1)),
            X0: (m_ref, B0, gai(0, 1)),
            X2: (mv.at[A2], B2, gai(0, 1)),
        }[flow]
        return remote(
            src.at[rows], mv.at[dst, rows], msend.at[flow, k], mrecv.at[flow, k], (target, ba)
        )

    @pl.loop(0, NCH)
    def _(k):
        hop(UP1, k).start()
        hop(DN1, k).start()
        hop(X0, k).start()

    own_p.wait()
    pp[...] = jnp.full(pp.shape, -1, jnp.int32)
    for a in range(16):
        pp[:, a * 128 : a * 128 + 126] = pairs[:, a * 126 : (a + 1) * 126]
    band = lax.rem(lax.broadcasted_iota(jnp.int32, (128, 2048), 0), 64)
    one_n[...] = jnp.where(band == pp[1:2, :], 1.0, 0.0).astype(jnp.bfloat16)
    facc[...] = jnp.zeros_like(facc)

    def pieces(index, first, count, sems, device):
        part = wf.at[pl.ds(first, count)]
        return remote(part, part, sems[0].at[index], sems[1].at[index], device)

    def arrived(index, first, count):
        part = wf.at[pl.ds(first, count)]
        remote(part, part, w2s.at[index], w2r.at[index], (ga, ba)).wait_recv()

    sems2, sems3 = (w2s, w2r), (w3s, w3r)
    other = (ga, bai(0, 0, 1 - c))
    up_y, down_y = (ga, bai(1, 0, c)), (ga, bai(-1, 0, c))
    base = (c * 4 + y) * 2
    base_up = (c * 4 + lax.rem(y + 1, 4)) * 2
    base_down = (c * 4 + lax.rem(y + 3, 4)) * 2
    base_far = (c * 4 + lax.rem(y + 2, 4)) * 2
    sends = []

    def launch(cp):
        cp.start()
        sends.append(cp)

    def fwd(k):
        hop(UP1, k).wait_recv()
        hop(UP2, k).start()
        hop(DN1, k).wait_recv()
        hop(DN2, k).start()

    lane = lax.broadcasted_iota(jnp.int32, (64, 128), 1) // 64

    def accumulate(per_band, first_band):
        for f in range(2):
            total = facc[pl.ds(f * 64, 64), :]
            for q in range(per_band.shape[0] // 64):
                part = per_band[q * 64 : (q + 1) * 64, (q // 2) * 128 : (q // 2 + 1) * 128]
                total += jnp.where(lane == q % 2, part * bf_ref[f, first_band + q], 0.0)
            facc[pl.ds(f * 64, 64), :] = total

    def by_column(applied, right):
        high, low = halves(applied)
        return dot_nt(high, right) + dot_nt(low, right)

    def by_row(left, turned):
        high, low = halves(turned)
        return dot(left, high) + dot(left, low)

    def block(index):
        return wf[:, index].reshape(GB, GB)

    def early(e):
        rows = pl.ds(pl.multiple_of(e * 256, 256), 256)
        hop(X0, 2 * e).wait_recv()
        hop(X0, 2 * e + 1).wait_recv()
        a0 = mv[A0, rows, :]
        applied = dot(a0, wown[A0])
        for slot in (A1, AM1, B0):
            applied += dot(mv[slot, rows, :], wown[slot])
        accumulate(by_column(applied, a0), 4 * e)
        t2[:, rows] = dot_nt(wown[A2], a0)
        tm2[:, rows] = dot_nt(wown[AM2], a0)
        tb2[:, rows] = dot_nt(wown[B2], a0)

    def middle(e):
        rows = pl.ds(pl.multiple_of(e * 256, 256), 256)
        am1, a1, b0 = mv[AM1, rows, :], mv[A1, rows, :], mv[B0, rows, :]
        accumulate(by_column(dot(am1, block(0)) + dot(a1, block(1)), b0), 4 * e)
        tm2[:, rows] += dot_nt(block(2), b0) + dot_nt(block(3), a1)
        t2[:, rows] += dot_nt(block(4), am1)
        tb2[:, rows] += dot_nt(block(5), am1)
        ab2[rows, :] = dot(am1, block(8))

    def late(k):
        rows = pl.ds(pl.multiple_of(k * CH, CH), CH)
        hop(UP2, k).wait_recv()
        am2 = mv[AM2, rows, :]
        tb2[:, rows] += dot_nt(block(7), am2)
        turned = t2[:, rows] + dot_nt(block(6), am2)
        accumulate(by_row(mv[A2, rows, :], turned) + by_row(am2, tm2[:, rows]), 2 * k)

    def last(k):
        rows = pl.ds(pl.multiple_of(k * CH, CH), CH)
        hop(X2, k).wait_recv()
        b2 = mv[B2, rows, :]
        accumulate(by_row(b2, tb2[:, rows]) + by_column(ab2[rows, :], b2), 2 * k)

    wait_bytes(wf.at[mine_w], w1r)
    launch(pieces(0, mine_w, 1, sems2, (ga, bai(0, 1, c))))
    fwd(0)
    arrived(0, share(0, 1, c), 1)
    launch(pieces(1, base, 2, sems2, up_y))
    launch(pieces(2, base, 2, sems2, down_y))
    launch(pieces(0, base, 2, sems3, other))
    fwd(1)
    own_m.wait()
    for cp in own_w:
        cp.wait()

    @pl.loop(0, 2)
    def _(e):
        fwd(2 * e + 2)
        fwd(2 * e + 3)
        early(e)

    arrived(1, base_down, 2)
    launch(pieces(3, base_down, 1, sems2, up_y))
    launch(pieces(1, base_down, 2, sems3, other))
    arrived(2, base_up, 2)
    launch(pieces(4, base_up + 1, 1, sems2, down_y))
    launch(pieces(2, base_up, 2, sems3, other))

    fwd(6)
    fwd(7)

    @pl.loop(2, 4)
    def _(e):
        early(e)

    arrived(3, base_far, 1)
    launch(pieces(3, base_far, 1, sems3, other))
    arrived(4, base_far + 1, 1)
    launch(pieces(4, base_far + 1, 1, sems3, other))
    mirror = (1 - 2 * c) * 8
    for index, first, count in (
        (0, base, 2), (1, base_down, 2), (2, base_up, 2), (3, base_far, 1), (4, base_far + 1, 1),
    ):
        part = wf.at[pl.ds(first + mirror, count)]
        remote(part, part, w3s.at[index], w3r.at[index], other).wait_recv()

    @pl.loop(0, NCH + 1)
    def _(k):
        @pl.when(k < NCH)
        def _():
            hop(DN2, k).wait_recv()
            hop(X2, k).start()

            @pl.when(lax.rem(k, 2) == 0)
            def _():
                middle(k // 2)

            late(k)

        @pl.when(k >= 1)
        def _():
            last(k - 1)

    full = facc[...]
    x1 = full.astype(jnp.bfloat16)
    rest = full - x1.astype(jnp.float32)
    x2 = rest.astype(jnp.bfloat16)
    x3 = (rest - x2.astype(jnp.float32)).astype(jnp.bfloat16)
    picked = (
        jnp.dot(x1, one_n[...], preferred_element_type=jnp.float32)
        + jnp.dot(x2, one_n[...], preferred_element_type=jnp.float32)
        + jnp.dot(x3, one_n[...], preferred_element_type=jnp.float32)
    )
    first = lax.broadcasted_iota(jnp.int32, (64, 2048), 0) == pp[0:1, :]
    for f in range(2):
        row = jnp.sum(jnp.where(first, picked[f * 64 : (f + 1) * 64], 0.0), axis=0, keepdims=True)
        for a in range(16):
            red_src[a, f : f + 1, :] = row[:, a * 128 : (a + 1) * 128]

    @pl.loop(1, 16)
    def _(k):
        peer = lax.rem(ga + k, 16)
        remote(red_src.at[peer], red_a.at[k - 1], r1s, r1r, (peer, ba)).start()

    wait_bytes(red_a, r1r)
    mine = red_src[ga]
    for k in range(15):
        mine += red_a[k]
    red_b[ba] = mine

    @pl.loop(1, 16)
    def _(k):
        peer = lax.rem(ba + k, 16)
        remote(red_b.at[ba], red_b.at[ba], r2s, r2r, (ga, peer)).start()

    wait_bytes(red_b.at[pl.ds(0, 15)], r2r)
    total = red_b[0]
    for k in range(1, 16):
        total += red_b[k]
    out_ref[...] = total[:, :126]

    wait_bytes(wf.at[0], w1s)
    for cp in sends:
        cp.wait_send()

    @pl.loop(0, NCH)
    def _(k):
        for flow in (UP1, DN1, UP2, DN2, X0, X2):
            hop(flow, k).wait_send()

    wait_bytes(red_a, r1s)
    wait_bytes(red_b.at[pl.ds(0, 15)], r2s)


def shards(matrix_elements, screening, band_factor, pair_list):
    bands, quasi, width = matrix_elements.shape
    dma = pltpu.SemaphoreType.DMA
    return pl.pallas_call(
        kernel,
        out_shape=jax.ShapeDtypeStruct((2, 126), jnp.float32),
        in_specs=[
            pl.BlockSpec(memory_space=pltpu.HBM),
            pl.BlockSpec(memory_space=pltpu.HBM),
            pl.BlockSpec(memory_space=pltpu.SMEM),
            pl.BlockSpec(memory_space=pltpu.HBM),
        ],
        out_specs=pl.BlockSpec(memory_space=pltpu.VMEM),
        scratch_shapes=[
            pltpu.VMEM((7, 1024, GB), jnp.bfloat16),
            pltpu.VMEM((7, GB, GB), jnp.bfloat16),
            pltpu.VMEM((16, NBLK, 32, GB), jnp.bfloat16),
            pltpu.VMEM((GB, 1024), jnp.float32),
            pltpu.VMEM((GB, 1024), jnp.float32),
            pltpu.VMEM((GB, 1024), jnp.float32),
            pltpu.VMEM((1024, GB), jnp.float32),
            pltpu.VMEM((2, 2016), jnp.int32),
            pltpu.VMEM((2, 2048), jnp.int32),
            pltpu.VMEM((128, 2048), jnp.bfloat16),
            pltpu.VMEM((128, 128), jnp.float32),
            pltpu.VMEM((16, 2, 128), jnp.float32),
            pltpu.VMEM((15, 2, 128), jnp.float32),
            pltpu.VMEM((16, 2, 128), jnp.float32),
            dma((6, NCH)), dma((6, NCH)), dma, dma((7,)), dma,
            dma, dma, dma((5,)), dma((5,)), dma((5,)), dma((5,)),
            dma, dma, dma, dma,
        ],
        compiler_params=pltpu.CompilerParams(
            collective_id=0, has_side_effects=True, vmem_limit_bytes=56 << 20
        ),
        cost_estimate=pl.CostEstimate(flops=9 * 10**9, bytes_accessed=20 << 20, transcendentals=0),
        name="self_energy",
    )(matrix_elements.reshape(bands * quasi, width), screening, band_factor, pair_list)


def solution(mesh):
    placed = (P("ba", None, "ga"), P(None, "ga"), P(None, "ba"), P())
    return jax.shard_map(
        shards, mesh=mesh, in_specs=placed, out_specs=P(None, "ga"), check_vma=False
    )
```

```python
import functools

import jax
import jax.numpy as jnp
from jax import lax
from jax.experimental import pallas as pl
from jax.experimental.pallas import tpu as pltpu
from jax.sharding import PartitionSpec as P

MESH = pl.DeviceIdType.MESH
GB = 512
CH = 128
NCH = 8
NBLK = 9
A0, A1, AM1, A2, AM2, B0, B2 = range(7)
UP1, UP2, DN1, DN2, X0, X2 = range(6)
NT = (((1,), (1,)), ((), ()))


def remote(src, dst, send, recv, device):
    return pltpu.make_async_remote_copy(
        src_ref=src, dst_ref=dst, send_sem=send, recv_sem=recv, device_id=device, device_id_type=MESH
    )


def wait_bytes(ref, sem):
    pltpu.make_async_copy(ref, ref, sem).wait()


def dot(a, b):
    return jnp.dot(a, b, preferred_element_type=jnp.float32)


def dot_nt(a, b):
    return lax.dot_general(a, b, NT, preferred_element_type=jnp.float32)


def halves(x):
    high = x.astype(jnp.bfloat16)
    return high, (x - high.astype(jnp.float32)).astype(jnp.bfloat16)


def kernel(
    m_ref, w_ref, bf_ref, pair_ref, out_ref,
    mv, wown, wf, t2, tm2, tb2, ab2, pairs, pp, one_n, facc, red_src, red_a, red_b,
    msend, mrecv, mloc, wloc, ploc, w1s, w1r, w2s, w2r, w3s, w3r, r1s, r1r, r2s, r2r,
):
    ga, ba = lax.axis_index("ga"), lax.axis_index("ba")
    z, s = ga // 2, lax.rem(ga, 2)
    y, xh, c = ba // 4, lax.rem(ba // 2, 2), lax.rem(ba, 2)

    def gai(dz, flip=0):
        side = 1 - s if flip else s
        return lax.rem(z + 8 + dz, 8) * 2 + side

    def bai(dy, dx, core):
        return (lax.rem(y + 4 + dy, 4) * 2 + lax.rem(xh + dx, 2)) * 2 + core

    def share(dy, dx, core):
        return (core * 4 + lax.rem(y + 4 + dy, 4)) * 2 + lax.rem(xh + dx, 2)

    barrier = pltpu.get_barrier_semaphore()

    @pl.loop(1, 16)
    def _(k):
        pl.semaphore_signal(barrier, inc=1, device_id=(lax.rem(ga + k, 16), ba), device_id_type=MESH)
        pl.semaphore_signal(barrier, inc=1, device_id=(ga, lax.rem(ba + k, 16)), device_id_type=MESH)

    own_p = pltpu.make_async_copy(pair_ref, pairs, ploc)
    own_p.start()
    own_m = pltpu.make_async_copy(m_ref, mv.at[A0], mloc)
    own_m.start()
    own_rows = (
        (A0, gai(0)), (A1, gai(1)), (AM1, gai(-1)), (A2, gai(2)), (AM2, gai(-2)),
        (B0, gai(0, 1)), (B2, gai(2, 1)),
    )
    own_w = []
    for slot, block in own_rows:
        cp = pltpu.make_async_copy(w_ref.at[pl.ds(block * GB, GB)], wown.at[slot], wloc.at[slot])
        cp.start()
        own_w.append(cp)

    pl.semaphore_wait(barrier, 30)

    mine_w = share(0, 0, c)
    plan = (
        (gai(2), ((gai(4), 6), (gai(4, 1), 7))),
        (gai(-2, 1), ((gai(-3, 1), 8),)),
        (gai(1), ((gai(3), 4), (gai(3, 1), 5))),
        (gai(-1), ((gai(-3), 3),)),
        (gai(0, 1), ((gai(-1, 1), 0), (gai(1, 1), 1), (gai(-2, 1), 2))),
    )
    for target, blocks in plan:
        for block, index in blocks:
            remote(
                w_ref.at[pl.ds(block * GB + mine_w * 32, 32)], wf.at[mine_w, index], w1s, w1r, (target, ba)
            ).start()

    def hop(flow, k):
        rows = pl.ds(pl.multiple_of(k * CH, CH), CH)
        src, dst, target = {
            UP1: (m_ref, AM1, gai(1)),
            DN1: (m_ref, A1, gai(-1)),
            UP2: (mv.at[AM1], AM2, gai(1)),
            DN2: (mv.at[A1], A2, gai(-1)),
            X0: (m_ref, B0, gai(0, 1)),
            X2: (mv.at[A2], B2, gai(0, 1)),
        }[flow]
        return remote(
            src.at[rows], mv.at[dst, rows], msend.at[flow, k], mrecv.at[flow, k], (target, ba)
        )

    @pl.loop(0, NCH)
    def _(k):
        hop(UP1, k).start()
        hop(DN1, k).start()

    own_p.wait()
    pp[...] = jnp.full(pp.shape, -1, jnp.int32)
    for a in range(16):
        pp[:, a * 128 : a * 128 + 126] = pairs[:, a * 126 : (a + 1) * 126]
    band = lax.rem(lax.broadcasted_iota(jnp.int32, (128, 2048), 0), 64)
    one_n[...] = jnp.where(band == pp[1:2, :], 1.0, 0.0).astype(jnp.bfloat16)
    facc[...] = jnp.zeros_like(facc)

    def pieces(index, first, count, sems, device):
        part = wf.at[pl.ds(first, count)]
        return remote(part, part, sems[0].at[index], sems[1].at[index], device)

    def arrived(index, first, count):
        part = wf.at[pl.ds(first, count)]
        remote(part, part, w2s.at[index], w2r.at[index], (ga, ba)).wait_recv()

    sems2, sems3 = (w2s, w2r), (w3s, w3r)
    other = (ga, bai(0, 0, 1 - c))
    up_y, down_y = (ga, bai(1, 0, c)), (ga, bai(-1, 0, c))
    base = (c * 4 + y) * 2
    base_up = (c * 4 + lax.rem(y + 1, 4)) * 2
    base_down = (c * 4 + lax.rem(y + 3, 4)) * 2
    base_far = (c * 4 + lax.rem(y + 2, 4)) * 2
    sends = []

    def launch(cp):
        cp.start()
        sends.append(cp)

    def fwd(k):
        hop(UP1, k).wait_recv()
        hop(UP2, k).start()
        hop(DN1, k).wait_recv()
        hop(DN2, k).start()

    lane = lax.broadcasted_iota(jnp.int32, (64, 128), 1) // 64

    def accumulate(per_band, first_band):
        for f in range(2):
            total = facc[pl.ds(f * 64, 64), :]
            for q in range(per_band.shape[0] // 64):
                part = per_band[q * 64 : (q + 1) * 64, (q // 2) * 128 : (q // 2 + 1) * 128]
                total += jnp.where(lane == q % 2, part * bf_ref[f, first_band + q], 0.0)
            facc[pl.ds(f * 64, 64), :] = total

    def by_column(applied, right):
        high, low = halves(applied)
        return dot_nt(high, right) + dot_nt(low, right)

    def by_row(left, turned):
        high, low = halves(turned)
        return dot(left, high) + dot(left, low)

    def block(index):
        return wf[:, index].reshape(GB, GB)

    def early(e):
        rows = pl.ds(pl.multiple_of(e * 256, 256), 256)
        hop(X0, 2 * e).wait_recv()
        hop(X0, 2 * e + 1).wait_recv()
        a0 = mv[A0, rows, :]
        applied = dot(a0, wown[A0])
        for slot in (A1, AM1, B0):
            applied += dot(mv[slot, rows, :], wown[slot])
        accumulate(by_column(applied, a0), 4 * e)
        t2[:, rows] = dot_nt(wown[A2], a0)
        tm2[:, rows] = dot_nt(wown[AM2], a0)
        tb2[:, rows] = dot_nt(wown[B2], a0)

    def middle(e):
        rows = pl.ds(pl.multiple_of(e * 256, 256), 256)
        am1, a1, b0 = mv[AM1, rows, :], mv[A1, rows, :], mv[B0, rows, :]
        accumulate(by_column(dot(am1, block(0)) + dot(a1, block(1)), b0), 4 * e)
        tm2[:, rows] += dot_nt(block(2), b0) + dot_nt(block(3), a1)
        t2[:, rows] += dot_nt(block(4), am1)
        tb2[:, rows] += dot_nt(block(5), am1)
        ab2[rows, :] = dot(am1, block(8))

    def late(k):
        rows = pl.ds(pl.multiple_of(k * CH, CH), CH)
        hop(UP2, k).wait_recv()
        am2 = mv[AM2, rows, :]
        tb2[:, rows] += dot_nt(block(7), am2)
        turned = t2[:, rows] + dot_nt(block(6), am2)
        accumulate(by_row(mv[A2, rows, :], turned) + by_row(am2, tm2[:, rows]), 2 * k)

    def last(k):
        rows = pl.ds(pl.multiple_of(k * CH, CH), CH)
        hop(X2, k).wait_recv()
        b2 = mv[B2, rows, :]
        accumulate(by_row(b2, tb2[:, rows]) + by_column(ab2[rows, :], b2), 2 * k)

    wait_bytes(wf.at[mine_w], w1r)
    launch(pieces(0, mine_w, 1, sems2, (ga, bai(0, 1, c))))

    @pl.loop(0, NCH)
    def _(k):
        hop(X0, k).start()

    fwd(0)
    arrived(0, share(0, 1, c), 1)
    launch(pieces(1, base, 2, sems2, up_y))
    launch(pieces(2, base, 2, sems2, down_y))
    launch(pieces(0, base, 2, sems3, other))
    fwd(1)
    own_m.wait()
    for cp in own_w:
        cp.wait()

    @pl.loop(0, 2)
    def _(e):
        fwd(2 * e + 2)
        fwd(2 * e + 3)
        early(e)

    arrived(1, base_down, 2)
    launch(pieces(3, base_down, 1, sems2, up_y))
    launch(pieces(1, base_down, 2, sems3, other))
    arrived(2, base_up, 2)
    launch(pieces(4, base_up + 1, 1, sems2, down_y))
    launch(pieces(2, base_up, 2, sems3, other))

    fwd(6)
    fwd(7)

    def cross(k):
        hop(DN2, k).wait_recv()
        hop(X2, k).start()

    cross(0)
    early(2)
    cross(1)
    early(3)
    cross(2)
    arrived(3, base_far, 1)
    launch(pieces(3, base_far, 1, sems3, other))
    arrived(4, base_far + 1, 1)
    launch(pieces(4, base_far + 1, 1, sems3, other))
    mirror = (1 - 2 * c) * 8
    for index, first, count in (
        (0, base, 2), (1, base_down, 2), (2, base_up, 2), (3, base_far, 1), (4, base_far + 1, 1),
    ):
        part = wf.at[pl.ds(first + mirror, count)]
        remote(part, part, w3s.at[index], w3r.at[index], other).wait_recv()

    @pl.loop(0, NCH + 1)
    def _(k):
        @pl.when(k + 3 < NCH)
        def _():
            cross(k + 3)

        @pl.when(k < NCH)
        def _():
            @pl.when(lax.rem(k, 2) == 0)
            def _():
                middle(k // 2)

            late(k)

        @pl.when(k >= 1)
        def _():
            last(k - 1)

    full = facc[...]
    x1 = full.astype(jnp.bfloat16)
    rest = full - x1.astype(jnp.float32)
    x2 = rest.astype(jnp.bfloat16)
    x3 = (rest - x2.astype(jnp.float32)).astype(jnp.bfloat16)
    picked = (
        jnp.dot(x1, one_n[...], preferred_element_type=jnp.float32)
        + jnp.dot(x2, one_n[...], preferred_element_type=jnp.float32)
        + jnp.dot(x3, one_n[...], preferred_element_type=jnp.float32)
    )
    first = lax.broadcasted_iota(jnp.int32, (64, 2048), 0) == pp[0:1, :]
    for f in range(2):
        row = jnp.sum(jnp.where(first, picked[f * 64 : (f + 1) * 64], 0.0), axis=0, keepdims=True)
        for a in range(16):
            red_src[a, f : f + 1, :] = row[:, a * 128 : (a + 1) * 128]

    @pl.loop(1, 16)
    def _(k):
        peer = lax.rem(ga + k, 16)
        remote(red_src.at[peer], red_a.at[k - 1], r1s, r1r, (peer, ba)).start()

    wait_bytes(red_a, r1r)
    mine = red_src[ga]
    for k in range(15):
        mine += red_a[k]
    red_b[ba] = mine

    @pl.loop(1, 16)
    def _(k):
        peer = lax.rem(ba + k, 16)
        remote(red_b.at[ba], red_b.at[ba], r2s, r2r, (ga, peer)).start()

    wait_bytes(red_b.at[pl.ds(0, 15)], r2r)
    total = red_b[0]
    for k in range(1, 16):
        total += red_b[k]
    out_ref[...] = total[:, :126]

    wait_bytes(wf.at[0], w1s)
    for cp in sends:
        cp.wait_send()

    @pl.loop(0, NCH)
    def _(k):
        for flow in (UP1, DN1, UP2, DN2, X0, X2):
            hop(flow, k).wait_send()

    wait_bytes(red_a, r1s)
    wait_bytes(red_b.at[pl.ds(0, 15)], r2s)


def shards(matrix_elements, screening, band_factor, pair_list):
    bands, quasi, width = matrix_elements.shape
    dma = pltpu.SemaphoreType.DMA
    return pl.pallas_call(
        kernel,
        out_shape=jax.ShapeDtypeStruct((2, 126), jnp.float32),
        in_specs=[
            pl.BlockSpec(memory_space=pltpu.HBM),
            pl.BlockSpec(memory_space=pltpu.HBM),
            pl.BlockSpec(memory_space=pltpu.SMEM),
            pl.BlockSpec(memory_space=pltpu.HBM),
        ],
        out_specs=pl.BlockSpec(memory_space=pltpu.VMEM),
        scratch_shapes=[
            pltpu.VMEM((7, 1024, GB), jnp.bfloat16),
            pltpu.VMEM((7, GB, GB), jnp.bfloat16),
            pltpu.VMEM((16, NBLK, 32, GB), jnp.bfloat16),
            pltpu.VMEM((GB, 1024), jnp.float32),
            pltpu.VMEM((GB, 1024), jnp.float32),
            pltpu.VMEM((GB, 1024), jnp.float32),
            pltpu.VMEM((1024, GB), jnp.float32),
            pltpu.VMEM((2, 2016), jnp.int32),
            pltpu.VMEM((2, 2048), jnp.int32),
            pltpu.VMEM((128, 2048), jnp.bfloat16),
            pltpu.VMEM((128, 128), jnp.float32),
            pltpu.VMEM((16, 2, 128), jnp.float32),
            pltpu.VMEM((15, 2, 128), jnp.float32),
            pltpu.VMEM((16, 2, 128), jnp.float32),
            dma((6, NCH)), dma((6, NCH)), dma, dma((7,)), dma,
            dma, dma, dma((5,)), dma((5,)), dma((5,)), dma((5,)),
            dma, dma, dma, dma,
        ],
        compiler_params=pltpu.CompilerParams(
            collective_id=0, has_side_effects=True, vmem_limit_bytes=56 << 20
        ),
        cost_estimate=pl.CostEstimate(flops=9 * 10**9, bytes_accessed=20 << 20, transcendentals=0),
        name="self_energy",
    )(matrix_elements.reshape(bands * quasi, width), screening, band_factor, pair_list)


def solution(mesh):
    placed = (P("ba", None, "ga"), P(None, "ga"), P(None, "ba"), P())
    return jax.shard_map(
        shards, mesh=mesh, in_specs=placed, out_specs=P(None, "ga"), check_vma=False
    )
```

```python
import functools

import jax
import jax.numpy as jnp
from jax import lax
from jax.experimental import pallas as pl
from jax.experimental.pallas import tpu as pltpu
from jax.sharding import PartitionSpec as P

MESH = pl.DeviceIdType.MESH
GB = 512
CH = 128
NCH = 8
NBLK = 9
A0, A1, AM1, A2, AM2, B0, B2 = range(7)
UP1, UP2, DN1, DN2, X0, X2 = range(6)
FAR_FIRST = (8, 9, 7, 10, 6, 11, 5, 12, 4, 13, 3, 14, 2, 15, 1)
NT = (((1,), (1,)), ((), ()))


def remote(src, dst, send, recv, device):
    return pltpu.make_async_remote_copy(
        src_ref=src, dst_ref=dst, send_sem=send, recv_sem=recv, device_id=device, device_id_type=MESH
    )


def wait_bytes(ref, sem):
    pltpu.make_async_copy(ref, ref, sem).wait()


def dot(a, b):
    return jnp.dot(a, b, preferred_element_type=jnp.float32)


def dot_nt(a, b):
    return lax.dot_general(a, b, NT, preferred_element_type=jnp.float32)


def halves(x):
    high = x.astype(jnp.bfloat16)
    return high, (x - high.astype(jnp.float32)).astype(jnp.bfloat16)


def kernel(
    m_ref, w_ref, bf_ref, pair_ref, out_ref,
    mv, wown, wf, t2, tm2, tb2, ab2, pairs, pp, one_n, facc, red_src, red_a, red_b,
    msend, mrecv, mloc, wloc, ploc, w1s, w1r, w2s, w2r, w3s, w3r, r1s, r1r, r2s, r2r,
):
    ga, ba = lax.axis_index("ga"), lax.axis_index("ba")
    z, s = ga // 2, lax.rem(ga, 2)
    y, xh, c = ba // 4, lax.rem(ba // 2, 2), lax.rem(ba, 2)

    def gai(dz, flip=0):
        side = 1 - s if flip else s
        return lax.rem(z + 8 + dz, 8) * 2 + side

    def bai(dy, dx, core):
        return (lax.rem(y + 4 + dy, 4) * 2 + lax.rem(xh + dx, 2)) * 2 + core

    barrier = pltpu.get_barrier_semaphore()

    @pl.loop(1, 16)
    def _(k):
        pl.semaphore_signal(barrier, inc=1, device_id=(lax.rem(ga + k, 16), ba), device_id_type=MESH)
        pl.semaphore_signal(barrier, inc=1, device_id=(ga, lax.rem(ba + k, 16)), device_id_type=MESH)

    own_p = pltpu.make_async_copy(pair_ref, pairs, ploc)
    own_p.start()
    own_m = pltpu.make_async_copy(m_ref, mv.at[A0], mloc)
    own_m.start()
    own_rows = (
        (A0, gai(0)), (A1, gai(1)), (AM1, gai(-1)), (A2, gai(2)), (AM2, gai(-2)),
        (B0, gai(0, 1)), (B2, gai(2, 1)),
    )
    own_w = []
    for slot, block in own_rows:
        cp = pltpu.make_async_copy(w_ref.at[pl.ds(block * GB, GB)], wown.at[slot], wloc.at[slot])
        cp.start()
        own_w.append(cp)

    pl.semaphore_wait(barrier, 30)

    here = c * 4 + y
    plan = (
        (gai(0, 1), ((gai(-1, 1), 0), (gai(1, 1), 1), (gai(-2, 1), 2))),
        (gai(-1), ((gai(-3), 3),)),
        (gai(1), ((gai(3), 4), (gai(3, 1), 5))),
        (gai(2), ((gai(4), 6), (gai(4, 1), 7))),
        (gai(-2, 1), ((gai(-3, 1), 8),)),
    )
    for target, blocks in plan:
        for block, index in blocks:
            h = index // 5
            remote(
                w_ref.at[pl.ds(block * GB + here * 64, 64)], wf.at[here, index],
                w1s.at[h], w1r.at[h], (target, ba),
            ).start()

    def hop(flow, k):
        size = CH // 2 if flow in (DN2, X2) else CH
        rows = pl.ds(pl.multiple_of(k * size, size), size)
        src, dst, target = {
            UP1: (m_ref, AM1, gai(1)),
            DN1: (m_ref, A1, gai(-1)),
            UP2: (mv.at[AM1], AM2, gai(1)),
            DN2: (mv.at[A1], A2, gai(-1)),
            X0: (m_ref, B0, gai(0, 1)),
            X2: (mv.at[A2], B2, gai(0, 1)),
        }[flow]
        return remote(
            src.at[rows], mv.at[dst, rows], msend.at[flow, k], mrecv.at[flow, k], (target, ba)
        )

    @pl.loop(0, NCH)
    def _(k):
        hop(UP1, k).start()
        hop(DN1, k).start()
        hop(X0, k).start()

    own_p.wait()
    pp[...] = jnp.full(pp.shape, -1, jnp.int32)
    for a in range(16):
        pp[:, a * 128 : a * 128 + 126] = pairs[:, a * 126 : (a + 1) * 126]
    band = lax.rem(lax.broadcasted_iota(jnp.int32, (128, 2048), 0), 64)
    one_n[...] = jnp.where(band == pp[1:2, :], 1.0, 0.0).astype(jnp.bfloat16)
    facc[...] = jnp.zeros_like(facc)

    up, down, far = c * 4 + lax.rem(y + 1, 4), c * 4 + lax.rem(y + 3, 4), c * 4 + lax.rem(y + 2, 4)
    up_y, down_y, other = (ga, bai(1, 0, c)), (ga, bai(-1, 0, c)), (ga, bai(0, 0, 1 - c))
    part = (pl.ds(0, 5), pl.ds(5, 4))
    sends = []

    def launch(cp):
        cp.start()
        sends.append(cp)

    def to_y(index, slot, h, device):
        view = wf.at[slot, part[h]]
        return remote(view, view, w2s.at[index], w2r.at[index], device)

    def to_core(index, slot, h):
        view = wf.at[slot, part[h]]
        return remote(view, view, w3s.at[index], w3r.at[index], other)

    def fwd(k):
        hop(UP1, k).wait_recv()
        hop(UP2, k).start()
        hop(DN1, k).wait_recv()
        hop(DN2, 2 * k).start()
        hop(DN2, 2 * k + 1).start()

    lane = lax.broadcasted_iota(jnp.int32, (64, 128), 1) // 64

    def accumulate(per_band, first_band):
        for f in range(2):
            total = facc[pl.ds(f * 64, 64), :]
            for q in range(per_band.shape[0] // 64):
                part = per_band[q * 64 : (q + 1) * 64, (q // 2) * 128 : (q // 2 + 1) * 128]
                total += jnp.where(lane == q % 2, part * bf_ref[f, first_band + q], 0.0)
            facc[pl.ds(f * 64, 64), :] = total

    def by_column(applied, right):
        high, low = halves(applied)
        return dot_nt(high, right) + dot_nt(low, right)

    def by_row(left, turned):
        high, low = halves(turned)
        return dot(left, high) + dot(left, low)

    def block(index):
        return wf[:, index].reshape(GB, GB)

    def early(e):
        rows = pl.ds(pl.multiple_of(e * 256, 256), 256)
        hop(X0, 2 * e).wait_recv()
        hop(X0, 2 * e + 1).wait_recv()
        a0 = mv[A0, rows, :]
        applied = dot(a0, wown[A0])
        for slot in (A1, AM1, B0):
            applied += dot(mv[slot, rows, :], wown[slot])
        accumulate(by_column(applied, a0), 4 * e)
        t2[:, rows] = dot_nt(wown[A2], a0)
        tm2[:, rows] = dot_nt(wown[AM2], a0)
        tb2[:, rows] = dot_nt(wown[B2], a0)

    def middle(e):
        rows = pl.ds(pl.multiple_of(e * 256, 256), 256)
        am1, a1, b0 = mv[AM1, rows, :], mv[A1, rows, :], mv[B0, rows, :]
        accumulate(by_column(dot(am1, block(0)) + dot(a1, block(1)), b0), 4 * e)
        tm2[:, rows] += dot_nt(block(2), b0) + dot_nt(block(3), a1)
        t2[:, rows] += dot_nt(block(4), am1)
        tb2[:, rows] += dot_nt(block(5), am1)
        ab2[rows, :] = dot(am1, block(8))

    def late(k):
        rows = pl.ds(pl.multiple_of(k * CH, CH), CH)
        hop(UP2, k).wait_recv()
        am2 = mv[AM2, rows, :]
        tb2[:, rows] += dot_nt(block(7), am2)
        turned = t2[:, rows] + dot_nt(block(6), am2)
        accumulate(by_row(mv[A2, rows, :], turned) + by_row(am2, tm2[:, rows]), 2 * k)

    def last(k):
        rows = pl.ds(pl.multiple_of(k * CH, CH), CH)
        hop(X2, 2 * k).wait_recv()
        hop(X2, 2 * k + 1).wait_recv()
        b2 = mv[B2, rows, :]
        accumulate(by_row(b2, tb2[:, rows]) + by_column(ab2[rows, :], b2), 2 * k)

    def cross(k):
        for h in range(2):
            hop(DN2, 2 * k + h).wait_recv()
            hop(X2, 2 * k + h).start()

    def gather_own(h):
        wait_bytes(wf.at[here, part[h]], w1r.at[h])
        launch(to_y(h, here, h, up_y))
        launch(to_y(2 + h, here, h, down_y))
        launch(to_core(h, here, h))

    def gather_near(h):
        to_y(h, down, h, up_y).wait_recv()
        if h == 0:
            launch(to_y(4, down, h, up_y))
        launch(to_core(2 + h, down, h))
        to_y(2 + h, up, h, up_y).wait_recv()
        if h == 1:
            launch(to_y(5, up, h, down_y))
        launch(to_core(4 + h, up, h))

    gather_own(0)
    fwd(0)
    gather_own(1)
    fwd(1)
    own_m.wait()
    for cp in own_w:
        cp.wait()
    gather_near(0)
    fwd(2)
    fwd(3)
    early(0)
    gather_near(1)
    fwd(4)
    fwd(5)
    early(1)
    to_y(4, far, 0, up_y).wait_recv()
    launch(to_core(6, far, 0))
    fwd(6)
    fwd(7)
    early(2)
    to_y(5, far, 1, up_y).wait_recv()
    launch(to_core(7, far, 1))
    cross(0)
    early(3)
    cross(1)
    mirror = (1 - 2 * c) * 4
    for index, slot in enumerate((here, here, down, down, up, up, far, far)):
        to_core(index, slot + mirror, index % 2).wait_recv()

    @pl.loop(0, NCH + 1)
    def _(k):
        @pl.when(k + 2 < NCH)
        def _():
            cross(k + 2)

        @pl.when(k >= 1)
        def _():
            last(k - 1)

        @pl.when(k < NCH // 2)
        def _():
            middle(k)

        @pl.when(k < NCH)
        def _():
            late(k)

    full = facc[...]
    x1 = full.astype(jnp.bfloat16)
    rest = full - x1.astype(jnp.float32)
    x2 = rest.astype(jnp.bfloat16)
    picked = dot(x1, one_n[...]) + dot(x2, one_n[...])
    first = lax.broadcasted_iota(jnp.int32, (64, 2048), 0) == pp[0:1, :]
    for f in range(2):
        row = jnp.sum(jnp.where(first, picked[f * 64 : (f + 1) * 64], 0.0), axis=0, keepdims=True)
        for a in range(16):
            red_src[a, f : f + 1, :] = row[:, a * 128 : (a + 1) * 128]

    for k in FAR_FIRST:
        peer = lax.rem(ga + k, 16)
        remote(red_src.at[peer], red_a.at[k - 1], r1s, r1r, (peer, ba)).start()

    for h in range(2):
        wait_bytes(wf.at[here, part[h]], w1s.at[h])
    for cp in sends:
        cp.wait_send()

    @pl.loop(0, NCH)
    def _(k):
        for flow in (UP1, DN1, UP2, X0):
            hop(flow, k).wait_send()
        for flow in (DN2, X2):
            hop(flow, 2 * k).wait_send()
            hop(flow, 2 * k + 1).wait_send()

    wait_bytes(red_a, r1r)
    mine = red_src[ga]
    for k in range(15):
        mine += red_a[k]
    red_b[ba] = mine

    for k in FAR_FIRST:
        peer = lax.rem(ba + k, 16)
        remote(red_b.at[ba], red_b.at[ba], r2s, r2r, (ga, peer)).start()

    wait_bytes(red_a, r1s)
    wait_bytes(red_b.at[pl.ds(0, 15)], r2r)
    total = red_b[0]
    for k in range(1, 16):
        total += red_b[k]
    out_ref[...] = total[:, :126]

    wait_bytes(red_b.at[pl.ds(0, 15)], r2s)


def shards(matrix_elements, screening, band_factor, pair_list):
    bands, quasi, width = matrix_elements.shape
    dma = pltpu.SemaphoreType.DMA
    return pl.pallas_call(
        kernel,
        out_shape=jax.ShapeDtypeStruct((2, 126), jnp.float32),
        in_specs=[
            pl.BlockSpec(memory_space=pltpu.HBM),
            pl.BlockSpec(memory_space=pltpu.HBM),
            pl.BlockSpec(memory_space=pltpu.SMEM),
            pl.BlockSpec(memory_space=pltpu.HBM),
        ],
        out_specs=pl.BlockSpec(memory_space=pltpu.VMEM),
        scratch_shapes=[
            pltpu.VMEM((7, 1024, GB), jnp.bfloat16),
            pltpu.VMEM((7, GB, GB), jnp.bfloat16),
            pltpu.VMEM((8, NBLK, 64, GB), jnp.bfloat16),
            pltpu.VMEM((GB, 1024), jnp.float32),
            pltpu.VMEM((GB, 1024), jnp.float32),
            pltpu.VMEM((GB, 1024), jnp.float32),
            pltpu.VMEM((1024, GB), jnp.float32),
            pltpu.VMEM((2, 2016), jnp.int32),
            pltpu.VMEM((2, 2048), jnp.int32),
            pltpu.VMEM((128, 2048), jnp.bfloat16),
            pltpu.VMEM((128, 128), jnp.float32),
            pltpu.VMEM((16, 2, 128), jnp.float32),
            pltpu.VMEM((15, 2, 128), jnp.float32),
            pltpu.VMEM((16, 2, 128), jnp.float32),
            dma((6, 2 * NCH)), dma((6, 2 * NCH)), dma, dma((7,)), dma,
            dma((2,)), dma((2,)), dma((6,)), dma((6,)), dma((8,)), dma((8,)),
            dma, dma, dma, dma,
        ],
        compiler_params=pltpu.CompilerParams(
            collective_id=0, has_side_effects=True, vmem_limit_bytes=44 << 20
        ),
        cost_estimate=pl.CostEstimate(flops=9 * 10**9, bytes_accessed=20 << 20, transcendentals=0),
        name="self_energy",
    )(matrix_elements.reshape(bands * quasi, width), screening, band_factor, pair_list)


def solution(mesh):
    placed = (P("ba", None, "ga"), P(None, "ga"), P(None, "ba"), P())
    return jax.shard_map(
        shards, mesh=mesh, in_specs=placed, out_specs=P(None, "ga"), check_vma=False
    )
```

```python
import functools

import jax
import jax.numpy as jnp
from jax import lax
from jax.experimental import pallas as pl
from jax.experimental.pallas import tpu as pltpu
from jax.sharding import PartitionSpec as P

MESH = pl.DeviceIdType.MESH
GB = 512
CH = 128
NCH = 8
NBLK = 9
A0, A1, AM1, A2, AM2, B0, B2 = range(7)
UP1, UP2, DN1, DN2, X0, X2 = range(6)
FAR_FIRST = (8, 9, 7, 10, 6, 11, 5, 12, 4, 13, 3, 14, 2, 15, 1)
NT = (((1,), (1,)), ((), ()))


def remote(src, dst, send, recv, device):
    return pltpu.make_async_remote_copy(
        src_ref=src, dst_ref=dst, send_sem=send, recv_sem=recv, device_id=device, device_id_type=MESH
    )


def wait_bytes(ref, sem):
    pltpu.make_async_copy(ref, ref, sem).wait()


def dot(a, b):
    return jnp.dot(a, b, preferred_element_type=jnp.float32)


def dot_nt(a, b):
    return lax.dot_general(a, b, NT, preferred_element_type=jnp.float32)


def halves(x):
    high = x.astype(jnp.bfloat16)
    return high, (x - high.astype(jnp.float32)).astype(jnp.bfloat16)


def kernel(
    m_ref, w_ref, bf_ref, pair_ref, out_ref,
    mv, wown, wf, t2, tm2, tb2, ab2, pairs, pp, one_n, facc, red_src, red_a, red_b,
    msend, mrecv, mloc, wloc, ploc, known, w1s, w1r, w2s, w2r, w3s, w3r, r1s, r1r, r2s, r2r,
):
    ga, ba = lax.axis_index("ga"), lax.axis_index("ba")
    z, s = ga // 2, lax.rem(ga, 2)
    y, xh, c = ba // 4, lax.rem(ba // 2, 2), lax.rem(ba, 2)

    def gai(dz, flip=0):
        side = 1 - s if flip else s
        return lax.rem(z + 8 + dz, 8) * 2 + side

    def bai(dy, dx, core):
        return (lax.rem(y + 4 + dy, 4) * 2 + lax.rem(xh + dx, 2)) * 2 + core

    barrier = pltpu.get_barrier_semaphore()

    neighbours = (
        (gai(1), ba), (gai(-1), ba), (gai(0, 1), ba), (gai(0, 1), bai(0, 1, c)),
        (ga, bai(1, 0, c)), (ga, bai(-1, 0, c)), (ga, bai(0, 0, 1 - c)),
    )

    def greet(sem):
        for device in neighbours:
            pl.semaphore_signal(sem, inc=1, device_id=device, device_id_type=MESH)

    greet(barrier)

    own_p = pltpu.make_async_copy(pair_ref, pairs, ploc)
    own_p.start()
    own_m = pltpu.make_async_copy(m_ref, mv.at[A0], mloc)
    own_m.start()
    own_rows = (
        (A0, gai(0)), (A1, gai(1)), (AM1, gai(-1)), (A2, gai(2)), (AM2, gai(-2)),
        (B0, gai(0, 1)), (B2, gai(2, 1)),
    )
    own_w = []
    for slot, block in own_rows:
        cp = pltpu.make_async_copy(w_ref.at[pl.ds(block * GB, GB)], wown.at[slot], wloc.at[slot])
        cp.start()
        own_w.append(cp)

    def hop(flow, k):
        size = CH // 2 if flow in (DN2, X2) else CH
        rows = pl.ds(pl.multiple_of(k * size, size), size)
        src, dst, target = {
            UP1: (m_ref, AM1, gai(1)),
            DN1: (m_ref, A1, gai(-1)),
            UP2: (mv.at[AM1], AM2, gai(1)),
            DN2: (mv.at[A1], A2, gai(-1)),
            X0: (m_ref, B0, gai(0, 1)),
            X2: (mv.at[A2], B2, gai(0, 1)),
        }[flow]
        return remote(
            src.at[rows], mv.at[dst, rows], msend.at[flow, k], mrecv.at[flow, k], (target, ba)
        )

    def first(k):
        hop(UP1, k).start()
        hop(DN1, k).start()
        hop(X0, k).start()

    here = c * 4 + y

    def give(target, *blocks):
        for block, index in blocks:
            h = index // 5
            remote(
                w_ref.at[pl.ds(block * GB + here * 64, 64)], wf.at[here, index],
                w1s.at[h], w1r.at[h], (target, ba),
            ).start()

    pl.semaphore_wait(barrier, 7)
    greet(known.at[0])
    first(0)
    give(gai(0, 1), (gai(-1, 1), 0), (gai(1, 1), 1), (gai(-2, 1), 2))
    give(gai(-1), (gai(-3), 3))
    give(gai(1), (gai(3), 4), (gai(3, 1), 5))
    pl.semaphore_wait(known.at[0], 7)
    greet(known.at[1])
    give(gai(2), (gai(4), 6), (gai(4, 1), 7))
    first(1)
    pl.semaphore_wait(known.at[1], 7)
    greet(known.at[2])
    give(gai(-2, 1), (gai(-3, 1), 8))

    @pl.loop(2, NCH)
    def _(k):
        first(k)

    own_p.wait()
    pp[...] = jnp.full(pp.shape, -1, jnp.int32)
    for a in range(16):
        pp[:, a * 128 : a * 128 + 126] = pairs[:, a * 126 : (a + 1) * 126]
    band = lax.rem(lax.broadcasted_iota(jnp.int32, (128, 2048), 0), 64)
    one_n[...] = jnp.where(band == pp[1:2, :], 1.0, 0.0).astype(jnp.bfloat16)
    facc[...] = jnp.zeros_like(facc)
    pl.semaphore_wait(known.at[2], 7)
    greet(known.at[3])

    up, down, far = c * 4 + lax.rem(y + 1, 4), c * 4 + lax.rem(y + 3, 4), c * 4 + lax.rem(y + 2, 4)
    up_y, down_y, other = (ga, bai(1, 0, c)), (ga, bai(-1, 0, c)), (ga, bai(0, 0, 1 - c))
    part = (pl.ds(0, 5), pl.ds(5, 4))
    sends = []

    def launch(cp):
        cp.start()
        sends.append(cp)

    def to_y(index, slot, h, device):
        view = wf.at[slot, part[h]]
        return remote(view, view, w2s.at[index], w2r.at[index], device)

    def to_core(index, slot, h):
        view = wf.at[slot, part[h]]
        return remote(view, view, w3s.at[index], w3r.at[index], other)

    def fwd(k):
        hop(UP1, k).wait_recv()
        hop(UP2, k).start()
        hop(DN1, k).wait_recv()
        hop(DN2, 2 * k).start()
        hop(DN2, 2 * k + 1).start()

    lane = lax.broadcasted_iota(jnp.int32, (64, 128), 1) // 64

    def accumulate(per_band, first_band):
        for f in range(2):
            total = facc[pl.ds(f * 64, 64), :]
            for q in range(per_band.shape[0] // 64):
                part = per_band[q * 64 : (q + 1) * 64, (q // 2) * 128 : (q // 2 + 1) * 128]
                total += jnp.where(lane == q % 2, part * bf_ref[f, first_band + q], 0.0)
            facc[pl.ds(f * 64, 64), :] = total

    def by_column(applied, right):
        high, low = halves(applied)
        return dot_nt(high, right) + dot_nt(low, right)

    def by_row(left, turned):
        high, low = halves(turned)
        return dot(left, high) + dot(left, low)

    def block(index):
        return wf[:, index].reshape(GB, GB)

    def early(e):
        rows = pl.ds(pl.multiple_of(e * 256, 256), 256)
        hop(X0, 2 * e).wait_recv()
        hop(X0, 2 * e + 1).wait_recv()
        a0 = mv[A0, rows, :]
        applied = dot(a0, wown[A0])
        for slot in (A1, AM1, B0):
            applied += dot(mv[slot, rows, :], wown[slot])
        accumulate(by_column(applied, a0), 4 * e)
        t2[:, rows] = dot_nt(wown[A2], a0)
        tm2[:, rows] = dot_nt(wown[AM2], a0)
        tb2[:, rows] = dot_nt(wown[B2], a0)

    def middle(e):
        rows = pl.ds(pl.multiple_of(e * 256, 256), 256)
        am1, a1, b0 = mv[AM1, rows, :], mv[A1, rows, :], mv[B0, rows, :]
        accumulate(by_column(dot(am1, block(0)) + dot(a1, block(1)), b0), 4 * e)
        tm2[:, rows] += dot_nt(block(2), b0) + dot_nt(block(3), a1)
        t2[:, rows] += dot_nt(block(4), am1)
        tb2[:, rows] += dot_nt(block(5), am1)
        ab2[rows, :] = dot(am1, block(8))

    def late(k):
        rows = pl.ds(pl.multiple_of(k * CH, CH), CH)
        hop(UP2, k).wait_recv()
        am2 = mv[AM2, rows, :]
        tb2[:, rows] += dot_nt(block(7), am2)
        turned = t2[:, rows] + dot_nt(block(6), am2)
        accumulate(by_row(mv[A2, rows, :], turned) + by_row(am2, tm2[:, rows]), 2 * k)

    def last(k):
        rows = pl.ds(pl.multiple_of(k * CH, CH), CH)
        hop(X2, 2 * k).wait_recv()
        hop(X2, 2 * k + 1).wait_recv()
        b2 = mv[B2, rows, :]
        accumulate(by_row(b2, tb2[:, rows]) + by_column(ab2[rows, :], b2), 2 * k)

    def cross(k):
        for h in range(2):
            hop(DN2, 2 * k + h).wait_recv()
            hop(X2, 2 * k + h).start()

    def gather_own(h):
        wait_bytes(wf.at[here, part[h]], w1r.at[h])
        launch(to_y(h, here, h, up_y))
        launch(to_y(2 + h, here, h, down_y))
        launch(to_core(h, here, h))

    def gather_near(h):
        to_y(h, down, h, up_y).wait_recv()
        if h == 0:
            launch(to_y(4, down, h, up_y))
        launch(to_core(2 + h, down, h))
        to_y(2 + h, up, h, up_y).wait_recv()
        if h == 1:
            launch(to_y(5, up, h, down_y))
        launch(to_core(4 + h, up, h))

    gather_own(0)
    fwd(0)
    gather_own(1)
    fwd(1)
    pl.semaphore_wait(known.at[3], 7)
    own_m.wait()
    for cp in own_w:
        cp.wait()
    gather_near(0)
    fwd(2)
    fwd(3)
    early(0)
    gather_near(1)
    fwd(4)
    fwd(5)
    early(1)
    to_y(4, far, 0, up_y).wait_recv()
    launch(to_core(6, far, 0))
    fwd(6)
    fwd(7)
    early(2)
    to_y(5, far, 1, up_y).wait_recv()
    launch(to_core(7, far, 1))
    cross(0)
    early(3)
    cross(1)
    mirror = (1 - 2 * c) * 4
    for index, slot in enumerate((here, here, down, down, up, up, far, far)):
        to_core(index, slot + mirror, index % 2).wait_recv()

    @pl.loop(0, NCH + 1)
    def _(k):
        @pl.when(k + 2 < NCH)
        def _():
            cross(k + 2)

        @pl.when(k >= 1)
        def _():
            last(k - 1)

        @pl.when(k < NCH // 2)
        def _():
            middle(k)

        @pl.when(k < NCH)
        def _():
            late(k)

    full = facc[...]
    x1 = full.astype(jnp.bfloat16)
    rest = full - x1.astype(jnp.float32)
    x2 = rest.astype(jnp.bfloat16)
    picked = dot(x1, one_n[...]) + dot(x2, one_n[...])
    one_m = lax.broadcasted_iota(jnp.int32, (64, 2048), 0) == pp[0:1, :]
    for f in range(2):
        row = jnp.sum(jnp.where(one_m, picked[f * 64 : (f + 1) * 64], 0.0), axis=0, keepdims=True)
        for a in range(16):
            red_src[a, f : f + 1, :] = row[:, a * 128 : (a + 1) * 128]

    for k in FAR_FIRST:
        peer = lax.rem(ga + k, 16)
        remote(red_src.at[peer], red_a.at[k - 1], r1s, r1r, (peer, ba)).start()

    for h in range(2):
        wait_bytes(wf.at[here, part[h]], w1s.at[h])
    for cp in sends:
        cp.wait_send()

    @pl.loop(0, NCH)
    def _(k):
        for flow in (UP1, DN1, UP2, X0):
            hop(flow, k).wait_send()
        for flow in (DN2, X2):
            hop(flow, 2 * k).wait_send()
            hop(flow, 2 * k + 1).wait_send()

    wait_bytes(red_a, r1r)
    mine = red_src[ga]
    for k in range(15):
        mine += red_a[k]
    red_b[ba] = mine

    for k in FAR_FIRST:
        peer = lax.rem(ba + k, 16)
        remote(red_b.at[ba], red_b.at[ba], r2s, r2r, (ga, peer)).start()

    wait_bytes(red_a, r1s)
    wait_bytes(red_b.at[pl.ds(0, 15)], r2r)
    total = red_b[0]
    for k in range(1, 16):
        total += red_b[k]
    out_ref[...] = total[:, :126]

    wait_bytes(red_b.at[pl.ds(0, 15)], r2s)


def shards(matrix_elements, screening, band_factor, pair_list):
    bands, quasi, width = matrix_elements.shape
    dma = pltpu.SemaphoreType.DMA
    return pl.pallas_call(
        kernel,
        out_shape=jax.ShapeDtypeStruct((2, 126), jnp.float32),
        in_specs=[
            pl.BlockSpec(memory_space=pltpu.HBM),
            pl.BlockSpec(memory_space=pltpu.HBM),
            pl.BlockSpec(memory_space=pltpu.SMEM),
            pl.BlockSpec(memory_space=pltpu.HBM),
        ],
        out_specs=pl.BlockSpec(memory_space=pltpu.VMEM),
        scratch_shapes=[
            pltpu.VMEM((7, 1024, GB), jnp.bfloat16),
            pltpu.VMEM((7, GB, GB), jnp.bfloat16),
            pltpu.VMEM((8, NBLK, 64, GB), jnp.bfloat16),
            pltpu.VMEM((GB, 1024), jnp.float32),
            pltpu.VMEM((GB, 1024), jnp.float32),
            pltpu.VMEM((GB, 1024), jnp.float32),
            pltpu.VMEM((1024, GB), jnp.float32),
            pltpu.VMEM((2, 2016), jnp.int32),
            pltpu.VMEM((2, 2048), jnp.int32),
            pltpu.VMEM((128, 2048), jnp.bfloat16),
            pltpu.VMEM((128, 128), jnp.float32),
            pltpu.VMEM((16, 2, 128), jnp.float32),
            pltpu.VMEM((15, 2, 128), jnp.float32),
            pltpu.VMEM((16, 2, 128), jnp.float32),
            dma((6, 2 * NCH)), dma((6, 2 * NCH)), dma, dma((7,)), dma,
            pltpu.SemaphoreType.REGULAR((4,)), dma((2,)), dma((2,)), dma((6,)), dma((6,)), dma((8,)), dma((8,)),
            dma, dma, dma, dma,
        ],
        compiler_params=pltpu.CompilerParams(
            collective_id=0, has_side_effects=True, vmem_limit_bytes=56 << 20
        ),
        cost_estimate=pl.CostEstimate(flops=9 * 10**9, bytes_accessed=20 << 20, transcendentals=0),
        name="self_energy",
    )(matrix_elements.reshape(bands * quasi, width), screening, band_factor, pair_list)


def solution(mesh):
    placed = (P("ba", None, "ga"), P(None, "ga"), P(None, "ba"), P())
    return jax.shard_map(
        shards, mesh=mesh, in_specs=placed, out_specs=P(None, "ga"), check_vma=False
    )
```

```python
import functools

import jax
import jax.numpy as jnp
from jax import lax
from jax.experimental import pallas as pl
from jax.experimental.pallas import tpu as pltpu
from jax.sharding import PartitionSpec as P

MESH = pl.DeviceIdType.MESH
GB = 512
CH = 128
NCH = 8
NEAR = 3
FAR = 6
A0, A1, AM1, A2, AM2, B0, B2 = range(7)
UP1, UP2, DN1, DN2, X0, X2 = range(6)
FAR_FIRST = (8, 9, 7, 10, 6, 11, 5, 12, 4, 13, 3, 14, 2, 15, 1)
NT = (((1,), (1,)), ((), ()))


def remote(src, dst, send, recv, device):
    return pltpu.make_async_remote_copy(
        src_ref=src, dst_ref=dst, send_sem=send, recv_sem=recv, device_id=device, device_id_type=MESH
    )


def wait_bytes(ref, sem):
    pltpu.make_async_copy(ref, ref, sem).wait()


def dot(a, b):
    return jnp.dot(a, b, preferred_element_type=jnp.float32)


def dot_nt(a, b):
    return lax.dot_general(a, b, NT, preferred_element_type=jnp.float32)


def halves(x):
    high = x.astype(jnp.bfloat16)
    return high, (x - high.astype(jnp.float32)).astype(jnp.bfloat16)


def kernel(
    m_ref, w_ref, bf_ref, pair_ref, out_ref,
    mv, wown, wn, wd, stage, t2, tm2, tb2, ab2, pairs, pp, one_n, facc, red_src, red_a, red_b,
    msend, mrecv, mloc, wloc, ploc, known, w1s, w1r, xs, xr, w2s, w2r, w3s, w3r, r1s, r1r, r2s, r2r,
):
    ga, ba = lax.axis_index("ga"), lax.axis_index("ba")
    z, s = ga // 2, lax.rem(ga, 2)
    y, xh, c = ba // 4, lax.rem(ba // 2, 2), lax.rem(ba, 2)

    def gai(dz, flip=0):
        side = 1 - s if flip else s
        return lax.rem(z + 8 + dz, 8) * 2 + side

    def bai(dy, dx, core):
        return (lax.rem(y + 4 + dy, 4) * 2 + lax.rem(xh + dx, 2)) * 2 + core

    barrier = pltpu.get_barrier_semaphore()

    neighbours = (
        (gai(1), ba), (gai(-1), ba), (gai(0, 1), ba), (gai(0, 1), bai(0, 1, c)),
        (ga, bai(1, 0, c)), (ga, bai(-1, 0, c)), (ga, bai(0, 0, 1 - c)),
    )

    def greet(sem):
        for device in neighbours:
            pl.semaphore_signal(sem, inc=1, device_id=device, device_id_type=MESH)

    greet(barrier)

    own_p = pltpu.make_async_copy(pair_ref, pairs, ploc)
    own_p.start()
    own_m = pltpu.make_async_copy(m_ref, mv.at[A0], mloc)
    own_m.start()
    own_rows = (
        (A0, gai(0)), (A1, gai(1)), (AM1, gai(-1)), (A2, gai(2)), (AM2, gai(-2)),
        (B0, gai(0, 1)), (B2, gai(2, 1)),
    )
    own_w = []
    for slot, block in own_rows:
        cp = pltpu.make_async_copy(w_ref.at[pl.ds(block * GB, GB)], wown.at[slot], wloc.at[slot])
        cp.start()
        own_w.append(cp)

    def hop(flow, k):
        size = CH // 2 if flow in (DN2, X2) else CH
        rows = pl.ds(pl.multiple_of(k * size, size), size)
        src, dst, target = {
            UP1: (m_ref, AM1, gai(1)),
            DN1: (m_ref, A1, gai(-1)),
            UP2: (mv.at[AM1], AM2, gai(1)),
            DN2: (mv.at[A1], A2, gai(-1)),
            X0: (m_ref, B0, gai(0, 1)),
            X2: (mv.at[A2], B2, gai(0, 1)),
        }[flow]
        return remote(
            src.at[rows], mv.at[dst, rows], msend.at[flow, k], mrecv.at[flow, k], (target, ba)
        )

    def first(k):
        hop(UP1, k).start()
        hop(DN1, k).start()
        if k < 5:
            hop(X0, k).start()

    here = c * 4 + y
    same, swap = xh, 1 - xh
    beyond = (gai(0, 1), bai(0, 1, c))

    def give_near(block, index):
        remote(
            w_ref.at[pl.ds(block * GB + here * 64, 64)], wn.at[here, index], w1s.at[0], w1r.at[0], beyond
        ).start()

    def give_far(device, piece, block, index):
        remote(
            w_ref.at[pl.ds(block * GB + piece * 32, 32)], wd.at[piece, index], w1s.at[1], w1r.at[1], device
        ).start()

    pl.semaphore_wait(barrier, 7)
    greet(known.at[0])
    first(0)
    own = here * 2 + same
    give_near(gai(-1, 1), 0)
    give_near(gai(1, 1), 1)
    give_near(gai(-2, 1), 2)
    give_far((gai(-1), ba), own, gai(-3), 0)
    give_far((gai(1), ba), own, gai(3), 1)
    give_far((gai(1), ba), own, gai(3, 1), 2)
    first(1)
    first(2)
    pl.semaphore_wait(known.at[0], 7)
    greet(known.at[1])
    give_far((gai(2), ba), own, gai(4), 3)
    give_far((gai(2), ba), own, gai(4, 1), 4)
    pl.semaphore_wait(known.at[1], 7)
    greet(known.at[2])
    give_far((gai(-2, 1), bai(0, 1, c)), here * 2 + swap, gai(-3, 1), 5)
    for k in range(3, NCH):
        first(k)

    own_p.wait()
    pp[...] = jnp.full(pp.shape, -1, jnp.int32)
    for a in range(16):
        pp[:, a * 128 : a * 128 + 126] = pairs[:, a * 126 : (a + 1) * 126]
    band = lax.rem(lax.broadcasted_iota(jnp.int32, (128, 2048), 0), 64)
    one_n[...] = jnp.where(band == pp[1:2, :], 1.0, 0.0).astype(jnp.bfloat16)
    facc[...] = jnp.zeros_like(facc)
    pl.semaphore_wait(known.at[2], 7)
    greet(known.at[3])

    up, down, over = c * 4 + lax.rem(y + 1, 4), c * 4 + lax.rem(y + 3, 4), c * 4 + lax.rem(y + 2, 4)
    up_y, down_y, other = (ga, bai(1, 0, c)), (ga, bai(-1, 0, c)), (ga, bai(0, 0, 1 - c))
    sends = []

    def launch(cp):
        cp.start()
        sends.append(cp)

    def to_y(index, view, device):
        return remote(view, view, w2s.at[index], w2r.at[index], device)

    def to_core(index, view):
        return remote(view, view, w3s.at[index], w3r.at[index], other)

    def x_first(h):
        part = pl.ds(3 * h, 3)
        return remote(wd.at[own, part], stage.at[part], xs.at[h], xr.at[h], beyond)

    def x_second(h):
        part = pl.ds(3 * h, 3)
        return remote(
            stage.at[part], wd.at[here * 2 + swap, part], xs.at[2 + h], xr.at[2 + h], (gai(0, 1), ba)
        )

    def fwd(k):
        hop(UP1, k).wait_recv()
        hop(UP2, k).start()
        hop(DN1, k).wait_recv()
        hop(DN2, 2 * k).start()
        hop(DN2, 2 * k + 1).start()

    lane = lax.broadcasted_iota(jnp.int32, (64, 128), 1) // 64

    def accumulate(per_band, first_band):
        for f in range(2):
            total = facc[pl.ds(f * 64, 64), :]
            for q in range(per_band.shape[0] // 64):
                part = per_band[q * 64 : (q + 1) * 64, (q // 2) * 128 : (q // 2 + 1) * 128]
                total += jnp.where(lane == q % 2, part * bf_ref[f, first_band + q], 0.0)
            facc[pl.ds(f * 64, 64), :] = total

    def by_column(applied, right):
        high, low = halves(applied)
        return dot_nt(high, right) + dot_nt(low, right)

    def by_row(left, turned):
        high, low = halves(turned)
        return dot(left, high) + dot(left, low)

    def block(index):
        if index < NEAR:
            return wn[:, index].reshape(GB, GB)
        return wd[:, index - NEAR].reshape(GB, GB)

    def early(e):
        rows = pl.ds(pl.multiple_of(e * 256, 256), 256)
        hop(X0, 2 * e).wait_recv()
        hop(X0, 2 * e + 1).wait_recv()
        a0 = mv[A0, rows, :]
        applied = dot(a0, wown[A0])
        for slot in (A1, AM1, B0):
            applied += dot(mv[slot, rows, :], wown[slot])
        accumulate(by_column(applied, a0), 4 * e)
        t2[:, rows] = dot_nt(wown[A2], a0)
        tm2[:, rows] = dot_nt(wown[AM2], a0)
        tb2[:, rows] = dot_nt(wown[B2], a0)

    def near(e):
        rows = pl.ds(pl.multiple_of(e * 256, 256), 256)
        am1, a1, b0 = mv[AM1, rows, :], mv[A1, rows, :], mv[B0, rows, :]
        accumulate(by_column(dot(am1, block(0)) + dot(a1, block(1)), b0), 4 * e)
        tm2[:, rows] += dot_nt(block(2), b0)

    def middle(e):
        rows = pl.ds(pl.multiple_of(e * 256, 256), 256)
        am1, a1 = mv[AM1, rows, :], mv[A1, rows, :]
        tm2[:, rows] += dot_nt(block(3), a1)
        t2[:, rows] += dot_nt(block(4), am1)
        tb2[:, rows] += dot_nt(block(5), am1)
        ab2[rows, :] = dot(am1, block(8))

    def late(k, count=1):
        rows = pl.ds(k * CH, count * CH)
        for j in range(count):
            hop(UP2, k + j).wait_recv()
        am2 = mv[AM2, rows, :]
        tb2[:, rows] += dot_nt(block(7), am2)
        turned = t2[:, rows] + dot_nt(block(6), am2)
        accumulate(by_row(mv[A2, rows, :], turned) + by_row(am2, tm2[:, rows]), 2 * k)

    def last(k, count=1):
        rows = pl.ds(k * CH, count * CH)
        for j in range(2 * count):
            hop(X2, 2 * k + j).wait_recv()
        b2 = mv[B2, rows, :]
        accumulate(by_row(b2, tb2[:, rows]) + by_column(ab2[rows, :], b2), 2 * k)

    def cross(k):
        for h in range(2):
            hop(DN2, 2 * k + h).wait_recv()
            hop(X2, 2 * k + h).start()

    wait_bytes(wn.at[here], w1r.at[0])
    launch(to_y(0, wn.at[here], up_y))
    launch(to_y(1, wn.at[here], down_y))
    launch(to_core(0, wn.at[here]))
    fwd(0)
    fwd(1)
    wait_bytes(wd.at[own], w1r.at[1])
    launch(x_first(0))
    launch(x_first(1))
    launch(to_y(3, wd.at[own], up_y))
    launch(to_y(4, wd.at[own], down_y))
    launch(to_core(4, wd.at[own]))
    fwd(2)
    hop(X0, 5).start()
    to_y(0, wn.at[down], up_y).wait_recv()
    launch(to_y(2, wn.at[down], up_y))
    launch(to_core(1, wn.at[down]))
    to_y(1, wn.at[up], up_y).wait_recv()
    launch(to_core(2, wn.at[up]))
    fwd(3)
    for h in range(2):
        x_first(h).wait_recv()
        launch(x_second(h))
    fwd(4)
    hop(X0, 6).start()
    hop(X0, 7).start()
    own_m.wait()
    for cp in own_w:
        cp.wait()
    early(0)
    to_y(3, wd.at[down * 2 + same], up_y).wait_recv()
    launch(to_y(7, wd.at[down * 2 + same], up_y))
    launch(to_core(5, wd.at[down * 2 + same]))
    to_y(4, wd.at[up * 2 + same], up_y).wait_recv()
    launch(to_core(6, wd.at[up * 2 + same]))
    fwd(5)
    early(1)
    to_y(2, wn.at[over], up_y).wait_recv()
    launch(to_core(3, wn.at[over]))
    fwd(6)
    mirror = (1 - 2 * c) * 4
    for index, slot in enumerate((here, down, up, over)):
        to_core(index, wn.at[slot + mirror]).wait_recv()
    near(0)
    fwd(7)
    x_second(0).wait_recv()
    x_second(1).wait_recv()
    launch(to_y(5, wd.at[here * 2 + swap], up_y))
    launch(to_y(6, wd.at[here * 2 + swap], down_y))
    launch(to_core(7, wd.at[here * 2 + swap]))
    to_y(7, wd.at[over * 2 + same], up_y).wait_recv()
    launch(to_core(8, wd.at[over * 2 + same]))
    near(1)
    cross(0)
    early(2)
    cross(1)
    to_y(6, wd.at[up * 2 + swap], up_y).wait_recv()
    launch(to_y(8, wd.at[up * 2 + swap], down_y))
    launch(to_core(9, wd.at[up * 2 + swap]))
    to_y(5, wd.at[down * 2 + swap], up_y).wait_recv()
    launch(to_core(10, wd.at[down * 2 + swap]))
    near(2)
    cross(2)
    pl.semaphore_wait(known.at[3], 7)
    early(3)
    cross(3)
    near(3)
    to_y(8, wd.at[over * 2 + swap], up_y).wait_recv()
    launch(to_core(11, wd.at[over * 2 + swap]))
    cross(4)
    for index, slot in enumerate((
        here * 2 + same, down * 2 + same, up * 2 + same, here * 2 + swap,
        over * 2 + same, up * 2 + swap, down * 2 + swap, over * 2 + swap,
    )):
        to_core(4 + index, wd.at[slot + 2 * mirror]).wait_recv()

    middle(0)
    middle(1)
    cross(5)
    middle(2)
    middle(3)
    late(0, 2)
    cross(6)
    late(2, 2)
    last(0, 2)
    late(4, 2)
    cross(7)
    last(2, 2)
    last(4, 2)
    late(6)
    last(6)
    late(7)
    last(7)

    full = facc[...]
    x1 = full.astype(jnp.bfloat16)
    rest = full - x1.astype(jnp.float32)
    x2 = rest.astype(jnp.bfloat16)
    picked = dot(x1, one_n[...]) + dot(x2, one_n[...])
    one_m = lax.broadcasted_iota(jnp.int32, (64, 2048), 0) == pp[0:1, :]
    for f in range(2):
        row = jnp.sum(jnp.where(one_m, picked[f * 64 : (f + 1) * 64], 0.0), axis=0, keepdims=True)
        for a in range(16):
            red_src[a, f : f + 1, :] = row[:, a * 128 : (a + 1) * 128]

    for k in FAR_FIRST:
        peer = lax.rem(ga + k, 16)
        remote(red_src.at[peer], red_a.at[k - 1], r1s, r1r, (peer, ba)).start()

    wait_bytes(wn.at[here], w1s.at[0])
    wait_bytes(wd.at[own], w1s.at[1])
    for cp in sends:
        cp.wait_send()

    @pl.loop(0, NCH)
    def _(k):
        for flow in (UP1, DN1, UP2, X0):
            hop(flow, k).wait_send()
        for flow in (DN2, X2):
            hop(flow, 2 * k).wait_send()
            hop(flow, 2 * k + 1).wait_send()

    wait_bytes(red_a, r1r)
    mine = red_src[ga]
    for k in range(15):
        mine += red_a[k]
    red_b[ba] = mine

    for k in FAR_FIRST:
        peer = lax.rem(ba + k, 16)
        remote(red_b.at[ba], red_b.at[ba], r2s, r2r, (ga, peer)).start()

    wait_bytes(red_a, r1s)
    wait_bytes(red_b.at[pl.ds(0, 15)], r2r)
    total = red_b[0]
    for k in range(1, 16):
        total += red_b[k]
    out_ref[...] = total[:, :126]

    wait_bytes(red_b.at[pl.ds(0, 15)], r2s)


def shards(matrix_elements, screening, band_factor, pair_list):
    bands, quasi, width = matrix_elements.shape
    dma = pltpu.SemaphoreType.DMA
    return pl.pallas_call(
        kernel,
        out_shape=jax.ShapeDtypeStruct((2, 126), jnp.float32),
        in_specs=[
            pl.BlockSpec(memory_space=pltpu.HBM),
            pl.BlockSpec(memory_space=pltpu.HBM),
            pl.BlockSpec(memory_space=pltpu.SMEM),
            pl.BlockSpec(memory_space=pltpu.HBM),
        ],
        out_specs=pl.BlockSpec(memory_space=pltpu.VMEM),
        scratch_shapes=[
            pltpu.VMEM((7, 1024, GB), jnp.bfloat16),
            pltpu.VMEM((7, GB, GB), jnp.bfloat16),
            pltpu.VMEM((8, NEAR, 64, GB), jnp.bfloat16),
            pltpu.VMEM((16, FAR, 32, GB), jnp.bfloat16),
            pltpu.VMEM((FAR, 32, GB), jnp.bfloat16),
            pltpu.VMEM((GB, 1024), jnp.float32),
            pltpu.VMEM((GB, 1024), jnp.float32),
            pltpu.VMEM((GB, 1024), jnp.float32),
            pltpu.VMEM((1024, GB), jnp.float32),
            pltpu.VMEM((2, 2016), jnp.int32),
            pltpu.VMEM((2, 2048), jnp.int32),
            pltpu.VMEM((128, 2048), jnp.bfloat16),
            pltpu.VMEM((128, 128), jnp.float32),
            pltpu.VMEM((16, 2, 128), jnp.float32),
            pltpu.VMEM((15, 2, 128), jnp.float32),
            pltpu.VMEM((16, 2, 128), jnp.float32),
            dma((6, 2 * NCH)), dma((6, 2 * NCH)), dma, dma((7,)), dma,
            pltpu.SemaphoreType.REGULAR((4,)), dma((2,)), dma((2,)), dma((4,)), dma((4,)), dma((9,)), dma((9,)), dma((12,)), dma((12,)),
            dma, dma, dma, dma,
        ],
        compiler_params=pltpu.CompilerParams(
            collective_id=0, has_side_effects=True, vmem_limit_bytes=56 << 20
        ),
        cost_estimate=pl.CostEstimate(flops=9 * 10**9, bytes_accessed=20 << 20, transcendentals=0),
        name="self_energy",
    )(matrix_elements.reshape(bands * quasi, width), screening, band_factor, pair_list)


def solution(mesh):
    placed = (P("ba", None, "ga"), P(None, "ga"), P(None, "ba"), P())
    return jax.shard_map(
        shards, mesh=mesh, in_specs=placed, out_specs=P(None, "ga"), check_vma=False
    )
```

```python
import functools

import jax
import jax.numpy as jnp
from jax import lax
from jax.experimental import pallas as pl
from jax.experimental.pallas import tpu as pltpu
from jax.sharding import PartitionSpec as P

MESH = pl.DeviceIdType.MESH
GB = 512
CH = 128
NCH = 8
NEAR = 3
FAR = 6
A0, A1, AM1, A2, AM2, B0, B2 = range(7)
UP1, UP2, DN1, DN2, X0, X2 = range(6)
FAR_FIRST = (8, 9, 7, 10, 6, 11, 5, 12, 4, 13, 3, 14, 2, 15, 1)
NT = (((1,), (1,)), ((), ()))


def remote(src, dst, send, recv, device):
    return pltpu.make_async_remote_copy(
        src_ref=src, dst_ref=dst, send_sem=send, recv_sem=recv, device_id=device, device_id_type=MESH
    )


def wait_bytes(ref, sem):
    pltpu.make_async_copy(ref, ref, sem).wait()


def dot(a, b):
    return jnp.dot(a, b, preferred_element_type=jnp.float32)


def dot_nt(a, b):
    return lax.dot_general(a, b, NT, preferred_element_type=jnp.float32)


def halves(x):
    high = x.astype(jnp.bfloat16)
    return high, (x - high.astype(jnp.float32)).astype(jnp.bfloat16)


def kernel(
    m_ref, w_ref, bf_ref, pair_ref, out_ref,
    mv, wown, wn, wd, stage, t2, tm2, tb2, ab2, pairs, pp, one_n, facc, red_src, red_a, red_b,
    msend, mrecv, mloc, wloc, ploc, known, w1s, w1r, xs, xr, w2s, w2r, w3s, w3r, r1s, r1r, r2s, r2r,
):
    ga, ba = lax.axis_index("ga"), lax.axis_index("ba")
    z, s = ga // 2, lax.rem(ga, 2)
    y, xh, c = ba // 4, lax.rem(ba // 2, 2), lax.rem(ba, 2)

    def gai(dz, flip=0):
        side = 1 - s if flip else s
        return lax.rem(z + 8 + dz, 8) * 2 + side

    def bai(dy, dx, core):
        return (lax.rem(y + 4 + dy, 4) * 2 + lax.rem(xh + dx, 2)) * 2 + core

    barrier = pltpu.get_barrier_semaphore()

    neighbours = (
        (gai(1), ba), (gai(-1), ba), (gai(0, 1), ba), (gai(0, 1), bai(0, 1, c)),
        (ga, bai(1, 0, c)), (ga, bai(-1, 0, c)), (ga, bai(0, 0, 1 - c)),
    )

    def greet(sem):
        for device in neighbours:
            pl.semaphore_signal(sem, inc=1, device_id=device, device_id_type=MESH)

    greet(barrier)

    own_p = pltpu.make_async_copy(pair_ref, pairs, ploc)
    own_p.start()
    own_m = pltpu.make_async_copy(m_ref, mv.at[A0], mloc)
    own_m.start()
    own_rows = (
        (A0, gai(0)), (A1, gai(1)), (AM1, gai(-1)), (A2, gai(2)), (AM2, gai(-2)),
        (B0, gai(0, 1)), (B2, gai(2, 1)),
    )
    own_w = []
    for slot, block in own_rows:
        cp = pltpu.make_async_copy(w_ref.at[pl.ds(block * GB, GB)], wown.at[slot], wloc.at[slot])
        cp.start()
        own_w.append(cp)

    def hop(flow, k):
        size = CH // 2 if flow in (DN2, X2) else CH
        rows = pl.ds(pl.multiple_of(k * size, size), size)
        src, dst, target = {
            UP1: (m_ref, AM1, gai(1)),
            DN1: (m_ref, A1, gai(-1)),
            UP2: (mv.at[AM1], AM2, gai(1)),
            DN2: (mv.at[A1], A2, gai(-1)),
            X0: (m_ref, B0, gai(0, 1)),
            X2: (mv.at[A2], B2, gai(0, 1)),
        }[flow]
        return remote(
            src.at[rows], mv.at[dst, rows], msend.at[flow, k], mrecv.at[flow, k], (target, ba)
        )

    def first(k):
        hop(UP1, k).start()
        hop(DN1, k).start()
        if k < 5:
            hop(X0, k).start()

    here = c * 4 + y
    same, swap = xh, 1 - xh
    beyond = (gai(0, 1), bai(0, 1, c))

    def give_near(block, index):
        remote(
            w_ref.at[pl.ds(block * GB + here * 64, 64)], wn.at[here, index], w1s.at[0], w1r.at[0], beyond
        ).start()

    def give_far(device, piece, block, index):
        remote(
            w_ref.at[pl.ds(block * GB + piece * 32, 32)], wd.at[piece, index], w1s.at[1], w1r.at[1], device
        ).start()

    pl.semaphore_wait(barrier, 7)
    greet(known.at[0])
    first(0)
    own = here * 2 + same
    give_near(gai(-1, 1), 0)
    give_near(gai(1, 1), 1)
    give_near(gai(-2, 1), 2)
    give_far((gai(-1), ba), own, gai(-3), 0)
    give_far((gai(1), ba), own, gai(3), 1)
    give_far((gai(1), ba), own, gai(3, 1), 2)
    pl.semaphore_wait(known.at[0], 7)
    greet(known.at[1])
    give_far((gai(2), ba), own, gai(4), 3)
    give_far((gai(2), ba), own, gai(4, 1), 4)
    first(1)
    pl.semaphore_wait(known.at[1], 7)
    greet(known.at[2])
    give_far((gai(-2, 1), bai(0, 1, c)), here * 2 + swap, gai(-3, 1), 5)
    for k in range(2, NCH):
        first(k)

    own_p.wait()
    pp[...] = jnp.full(pp.shape, -1, jnp.int32)
    for a in range(16):
        pp[:, a * 128 : a * 128 + 126] = pairs[:, a * 126 : (a + 1) * 126]
    band = lax.rem(lax.broadcasted_iota(jnp.int32, (128, 2048), 0), 64)
    one_n[...] = jnp.where(band == pp[1:2, :], 1.0, 0.0).astype(jnp.bfloat16)
    facc[...] = jnp.zeros_like(facc)
    pl.semaphore_wait(known.at[2], 7)
    greet(known.at[3])

    up, down, over = c * 4 + lax.rem(y + 1, 4), c * 4 + lax.rem(y + 3, 4), c * 4 + lax.rem(y + 2, 4)
    up_y, down_y, other = (ga, bai(1, 0, c)), (ga, bai(-1, 0, c)), (ga, bai(0, 0, 1 - c))
    sends = []

    def launch(cp):
        cp.start()
        sends.append(cp)

    def to_y(index, view, device):
        return remote(view, view, w2s.at[index], w2r.at[index], device)

    def to_core(index, view):
        return remote(view, view, w3s.at[index], w3r.at[index], other)

    def x_first(h):
        part = pl.ds(3 * h, 3)
        return remote(wd.at[own, part], stage.at[part], xs.at[h], xr.at[h], beyond)

    def x_second(h):
        part = pl.ds(3 * h, 3)
        return remote(
            stage.at[part], wd.at[here * 2 + swap, part], xs.at[2 + h], xr.at[2 + h], (gai(0, 1), ba)
        )

    def fwd(k):
        hop(UP1, k).wait_recv()
        hop(UP2, k).start()
        hop(DN1, k).wait_recv()
        hop(DN2, 2 * k).start()
        hop(DN2, 2 * k + 1).start()

    lane = lax.broadcasted_iota(jnp.int32, (64, 128), 1) // 64

    def accumulate(per_band, first_band):
        for f in range(2):
            total = facc[pl.ds(f * 64, 64), :]
            for q in range(per_band.shape[0] // 64):
                part = per_band[q * 64 : (q + 1) * 64, (q // 2) * 128 : (q // 2 + 1) * 128]
                total += jnp.where(lane == q % 2, part * bf_ref[f, first_band + q], 0.0)
            facc[pl.ds(f * 64, 64), :] = total

    def by_column(applied, right):
        high, low = halves(applied)
        return dot_nt(high, right) + dot_nt(low, right)

    def by_row(left, turned):
        high, low = halves(turned)
        return dot(left, high) + dot(left, low)

    def block(index):
        if index < NEAR:
            return wn[:, index].reshape(GB, GB)
        return wd[:, index - NEAR].reshape(GB, GB)

    def early(e):
        rows = pl.ds(pl.multiple_of(e * 256, 256), 256)
        hop(X0, 2 * e).wait_recv()
        hop(X0, 2 * e + 1).wait_recv()
        a0 = mv[A0, rows, :]
        applied = dot(a0, wown[A0])
        for slot in (A1, AM1, B0):
            applied += dot(mv[slot, rows, :], wown[slot])
        accumulate(by_column(applied, a0), 4 * e)
        t2[:, rows] = dot_nt(wown[A2], a0)
        tm2[:, rows] = dot_nt(wown[AM2], a0)
        tb2[:, rows] = dot_nt(wown[B2], a0)

    def near(e):
        rows = pl.ds(pl.multiple_of(e * 256, 256), 256)
        am1, a1, b0 = mv[AM1, rows, :], mv[A1, rows, :], mv[B0, rows, :]
        accumulate(by_column(dot(am1, block(0)) + dot(a1, block(1)), b0), 4 * e)
        tm2[:, rows] += dot_nt(block(2), b0)

    def middle(e):
        rows = pl.ds(pl.multiple_of(e * 256, 256), 256)
        am1, a1 = mv[AM1, rows, :], mv[A1, rows, :]
        tm2[:, rows] += dot_nt(block(3), a1)
        t2[:, rows] += dot_nt(block(4), am1)
        tb2[:, rows] += dot_nt(block(5), am1)
        ab2[rows, :] = dot(am1, block(8))

    def late(k, count=1):
        rows = pl.ds(k * CH, count * CH)
        for j in range(count):
            hop(UP2, k + j).wait_recv()
        am2 = mv[AM2, rows, :]
        tb2[:, rows] += dot_nt(block(7), am2)
        turned = t2[:, rows] + dot_nt(block(6), am2)
        accumulate(by_row(mv[A2, rows, :], turned) + by_row(am2, tm2[:, rows]), 2 * k)

    def last(k, count=1):
        rows = pl.ds(k * CH, count * CH)
        for j in range(2 * count):
            hop(X2, 2 * k + j).wait_recv()
        b2 = mv[B2, rows, :]
        accumulate(by_row(b2, tb2[:, rows]) + by_column(ab2[rows, :], b2), 2 * k)

    def cross(k):
        for h in range(2):
            hop(DN2, 2 * k + h).wait_recv()
            hop(X2, 2 * k + h).start()

    wait_bytes(wn.at[here], w1r.at[0])
    launch(to_y(0, wn.at[here], up_y))
    launch(to_y(1, wn.at[here], down_y))
    launch(to_core(0, wn.at[here]))
    fwd(0)
    fwd(1)
    wait_bytes(wd.at[own], w1r.at[1])
    launch(x_first(0))
    launch(x_first(1))
    launch(to_y(3, wd.at[own], up_y))
    launch(to_y(4, wd.at[own], down_y))
    launch(to_core(4, wd.at[own]))
    fwd(2)
    hop(X0, 5).start()
    to_y(0, wn.at[down], up_y).wait_recv()
    launch(to_y(2, wn.at[down], up_y))
    launch(to_core(1, wn.at[down]))
    to_y(1, wn.at[up], up_y).wait_recv()
    launch(to_core(2, wn.at[up]))
    fwd(3)
    for h in range(2):
        x_first(h).wait_recv()
        launch(x_second(h))
    fwd(4)
    hop(X0, 6).start()
    hop(X0, 7).start()
    own_m.wait()
    for cp in own_w:
        cp.wait()
    early(0)
    to_y(3, wd.at[down * 2 + same], up_y).wait_recv()
    launch(to_y(7, wd.at[down * 2 + same], up_y))
    launch(to_core(5, wd.at[down * 2 + same]))
    to_y(4, wd.at[up * 2 + same], up_y).wait_recv()
    launch(to_core(6, wd.at[up * 2 + same]))
    fwd(5)
    early(1)
    to_y(2, wn.at[over], up_y).wait_recv()
    launch(to_core(3, wn.at[over]))
    fwd(6)
    mirror = (1 - 2 * c) * 4
    for index, slot in enumerate((here, down, up, over)):
        to_core(index, wn.at[slot + mirror]).wait_recv()
    near(0)
    fwd(7)
    x_second(0).wait_recv()
    x_second(1).wait_recv()
    launch(to_y(5, wd.at[here * 2 + swap], up_y))
    launch(to_y(6, wd.at[here * 2 + swap], down_y))
    launch(to_core(7, wd.at[here * 2 + swap]))
    to_y(7, wd.at[over * 2 + same], up_y).wait_recv()
    launch(to_core(8, wd.at[over * 2 + same]))
    near(1)
    cross(0)
    early(2)
    cross(1)
    to_y(6, wd.at[up * 2 + swap], up_y).wait_recv()
    launch(to_y(8, wd.at[up * 2 + swap], down_y))
    launch(to_core(9, wd.at[up * 2 + swap]))
    to_y(5, wd.at[down * 2 + swap], up_y).wait_recv()
    launch(to_core(10, wd.at[down * 2 + swap]))
    near(2)
    cross(2)
    pl.semaphore_wait(known.at[3], 7)
    early(3)
    cross(3)
    near(3)
    to_y(8, wd.at[over * 2 + swap], up_y).wait_recv()
    launch(to_core(11, wd.at[over * 2 + swap]))
    cross(4)
    for index, slot in enumerate((
        here * 2 + same, down * 2 + same, up * 2 + same, here * 2 + swap,
        over * 2 + same, up * 2 + swap, down * 2 + swap, over * 2 + swap,
    )):
        to_core(4 + index, wd.at[slot + 2 * mirror]).wait_recv()

    middle(0)
    middle(1)
    cross(5)
    middle(2)
    late(0, 2)
    last(0, 2)
    cross(6)
    late(2, 2)
    middle(3)
    late(4, 2)
    cross(7)
    last(2, 2)
    late(6)
    last(4, 2)
    last(6)
    late(7)
    last(7)

    full = facc[...]
    x1 = full.astype(jnp.bfloat16)
    rest = full - x1.astype(jnp.float32)
    x2 = rest.astype(jnp.bfloat16)
    picked = dot(x1, one_n[...]) + dot(x2, one_n[...])
    one_m = lax.broadcasted_iota(jnp.int32, (64, 2048), 0) == pp[0:1, :]
    for f in range(2):
        row = jnp.sum(jnp.where(one_m, picked[f * 64 : (f + 1) * 64], 0.0), axis=0, keepdims=True)
        for a in range(16):
            red_src[a, f : f + 1, :] = row[:, a * 128 : (a + 1) * 128]

    for k in FAR_FIRST:
        peer = lax.rem(ga + k, 16)
        remote(red_src.at[peer], red_a.at[k - 1], r1s, r1r, (peer, ba)).start()

    wait_bytes(wn.at[here], w1s.at[0])
    wait_bytes(wd.at[own], w1s.at[1])
    for cp in sends:
        cp.wait_send()

    @pl.loop(0, NCH)
    def _(k):
        for flow in (UP1, DN1, UP2, X0):
            hop(flow, k).wait_send()
        for flow in (DN2, X2):
            hop(flow, 2 * k).wait_send()
            hop(flow, 2 * k + 1).wait_send()

    wait_bytes(red_a, r1r)
    mine = red_src[ga]
    for k in range(15):
        mine += red_a[k]
    red_b[...] = mine
    keep = pltpu.make_async_copy(red_b, out_ref.at[ba], ploc)
    keep.start()

    for k in FAR_FIRST:
        peer = lax.rem(ba + k, 16)
        remote(red_b, out_ref.at[ba], r2s, r2r, (ga, peer)).start()

    wait_bytes(red_a, r1s)
    keep.wait()
    wait_bytes(red_a, r2s)
    wait_bytes(out_ref.at[pl.ds(0, 15)], r2r)


def shards(matrix_elements, screening, band_factor, pair_list):
    bands, quasi, width = matrix_elements.shape
    dma = pltpu.SemaphoreType.DMA
    parts = pl.pallas_call(
        kernel,
        out_shape=jax.ShapeDtypeStruct((16, 2, 128), jnp.float32),
        in_specs=[
            pl.BlockSpec(memory_space=pltpu.HBM),
            pl.BlockSpec(memory_space=pltpu.HBM),
            pl.BlockSpec(memory_space=pltpu.SMEM),
            pl.BlockSpec(memory_space=pltpu.HBM),
        ],
        out_specs=pl.BlockSpec(memory_space=pltpu.HBM),
        scratch_shapes=[
            pltpu.VMEM((7, 1024, GB), jnp.bfloat16),
            pltpu.VMEM((7, GB, GB), jnp.bfloat16),
            pltpu.VMEM((8, NEAR, 64, GB), jnp.bfloat16),
            pltpu.VMEM((16, FAR, 32, GB), jnp.bfloat16),
            pltpu.VMEM((FAR, 32, GB), jnp.bfloat16),
            pltpu.VMEM((GB, 1024), jnp.float32),
            pltpu.VMEM((GB, 1024), jnp.float32),
            pltpu.VMEM((GB, 1024), jnp.float32),
            pltpu.VMEM((1024, GB), jnp.float32),
            pltpu.VMEM((2, 2016), jnp.int32),
            pltpu.VMEM((2, 2048), jnp.int32),
            pltpu.VMEM((128, 2048), jnp.bfloat16),
            pltpu.VMEM((128, 128), jnp.float32),
            pltpu.VMEM((16, 2, 128), jnp.float32),
            pltpu.VMEM((15, 2, 128), jnp.float32),
            pltpu.VMEM((2, 128), jnp.float32),
            dma((6, 2 * NCH)), dma((6, 2 * NCH)), dma, dma((7,)), dma,
            pltpu.SemaphoreType.REGULAR((4,)), dma((2,)), dma((2,)), dma((4,)), dma((4,)), dma((9,)), dma((9,)), dma((12,)), dma((12,)),
            dma, dma, dma, dma,
        ],
        compiler_params=pltpu.CompilerParams(
            collective_id=0, has_side_effects=True, vmem_limit_bytes=56 << 20
        ),
        cost_estimate=pl.CostEstimate(flops=9 * 10**9, bytes_accessed=20 << 20, transcendentals=0),
        name="self_energy",
    )(matrix_elements.reshape(bands * quasi, width), screening, band_factor, pair_list)
    return jnp.sum(parts, axis=0)[:, :126]


def solution(mesh):
    placed = (P("ba", None, "ga"), P(None, "ga"), P(None, "ba"), P())
    return jax.shard_map(
        shards, mesh=mesh, in_specs=placed, out_specs=P(None, "ga"), check_vma=False
    )
```

```python
import functools

import jax
import jax.numpy as jnp
from jax import lax
from jax.experimental import pallas as pl
from jax.experimental.pallas import tpu as pltpu
from jax.sharding import PartitionSpec as P

MESH = pl.DeviceIdType.MESH
GB = 512
CH = 128
NCH = 8
NEAR = 3
FAR = 6
A0, A1, AM1, A2, AM2, B0, B2 = range(7)
UP1, UP2, DN1, DN2, X0, X2 = range(6)
FAR_FIRST = (8, 9, 7, 10, 6, 11, 5, 12, 4, 13, 3, 14, 2, 15, 1)
NT = (((1,), (1,)), ((), ()))


def remote(src, dst, send, recv, device):
    return pltpu.make_async_remote_copy(
        src_ref=src, dst_ref=dst, send_sem=send, recv_sem=recv, device_id=device, device_id_type=MESH
    )


def wait_bytes(ref, sem):
    pltpu.make_async_copy(ref, ref, sem).wait()


def dot(a, b):
    return jnp.dot(a, b, preferred_element_type=jnp.float32)


def dot_nt(a, b):
    return lax.dot_general(a, b, NT, preferred_element_type=jnp.float32)


def halves(x):
    high = x.astype(jnp.bfloat16)
    return high, (x - high.astype(jnp.float32)).astype(jnp.bfloat16)


def kernel(
    m_ref, w_ref, factor_ref, pair_ref, out_ref,
    mv, wown, wn, wd, stage, t2, tm2, tb2, ab2, bf_ref, pairs, pp, one_n, facc, red_src, red_a, red_b,
    msend, mrecv, mloc, wloc, ploc, floc, known, w1s, w1r, xs, xr, w2s, w2r, w3s, w3r, r1s, r1r, r2s, r2r,
):
    ga, ba = lax.axis_index("ga"), lax.axis_index("ba")
    z, s = ga // 2, lax.rem(ga, 2)
    y, xh, c = ba // 4, lax.rem(ba // 2, 2), lax.rem(ba, 2)

    def gai(dz, flip=0):
        side = 1 - s if flip else s
        return lax.rem(z + 8 + dz, 8) * 2 + side

    def bai(dy, dx, core):
        return (lax.rem(y + 4 + dy, 4) * 2 + lax.rem(xh + dx, 2)) * 2 + core

    barrier = pltpu.get_barrier_semaphore()

    neighbours = (
        (gai(1), ba), (gai(-1), ba), (gai(0, 1), ba), (gai(0, 1), bai(0, 1, c)),
        (ga, bai(1, 0, c)), (ga, bai(-1, 0, c)), (ga, bai(0, 0, 1 - c)),
    )

    def greet(sem):
        for device in neighbours:
            pl.semaphore_signal(sem, inc=1, device_id=device, device_id_type=MESH)

    greet(barrier)

    def hop(flow, k):
        size = CH // 2 if flow in (DN2, X2) else CH
        rows = pl.ds(pl.multiple_of(k * size, size), size)
        src, dst, target = {
            UP1: (m_ref, AM1, gai(1)),
            DN1: (m_ref, A1, gai(-1)),
            UP2: (mv.at[AM1], AM2, gai(1)),
            DN2: (mv.at[A1], A2, gai(-1)),
            X0: (m_ref, B0, gai(0, 1)),
            X2: (mv.at[A2], B2, gai(0, 1)),
        }[flow]
        return remote(
            src.at[rows], mv.at[dst, rows], msend.at[flow, k], mrecv.at[flow, k], (target, ba)
        )

    def first(k):
        hop(UP1, k).start()
        hop(DN1, k).start()
        if k < 5:
            hop(X0, k).start()

    here = c * 4 + y
    same, swap = xh, 1 - xh
    beyond = (gai(0, 1), bai(0, 1, c))

    def give_near(block, index):
        remote(
            w_ref.at[pl.ds(block * GB + here * 64, 64)], wn.at[here, index], w1s.at[0], w1r.at[0], beyond
        ).start()

    def give_far(device, piece, block, index):
        remote(
            w_ref.at[pl.ds(block * GB + piece * 32, 32)], wd.at[piece, index], w1s.at[1], w1r.at[1], device
        ).start()

    pl.semaphore_wait(barrier, 7)
    first(0)
    greet(known.at[0])
    own = here * 2 + same
    give_near(gai(-1, 1), 0)
    give_near(gai(1, 1), 1)
    give_near(gai(-2, 1), 2)
    give_far((gai(-1), ba), own, gai(-3), 0)
    give_far((gai(1), ba), own, gai(3), 1)
    give_far((gai(1), ba), own, gai(3, 1), 2)
    pl.semaphore_wait(known.at[0], 7)
    greet(known.at[1])
    give_far((gai(2), ba), own, gai(4), 3)
    give_far((gai(2), ba), own, gai(4, 1), 4)
    first(1)
    pl.semaphore_wait(known.at[1], 7)
    greet(known.at[2])
    give_far((gai(-2, 1), bai(0, 1, c)), here * 2 + swap, gai(-3, 1), 5)
    for k in range(2, NCH):
        first(k)

    own_p = pltpu.make_async_copy(pair_ref, pairs, ploc)
    own_p.start()
    own_m = pltpu.make_async_copy(m_ref, mv.at[A0], mloc)
    own_m.start()
    own_rows = (
        (A0, gai(0)), (A1, gai(1)), (AM1, gai(-1)), (A2, gai(2)), (AM2, gai(-2)),
        (B0, gai(0, 1)), (B2, gai(2, 1)),
    )
    own_w = []
    for slot, block in own_rows:
        cp = pltpu.make_async_copy(w_ref.at[pl.ds(block * GB, GB)], wown.at[slot], wloc.at[slot])
        cp.start()
        own_w.append(cp)
    own_f = pltpu.make_async_copy(factor_ref, bf_ref, floc)
    own_f.start()

    own_p.wait()
    pp[...] = jnp.full(pp.shape, -1, jnp.int32)
    for a in range(16):
        pp[:, a * 128 : a * 128 + 126] = pairs[:, a * 126 : (a + 1) * 126]
    band = lax.rem(lax.broadcasted_iota(jnp.int32, (128, 2048), 0), 64)
    one_n[...] = jnp.where(band == pp[1:2, :], 1.0, 0.0).astype(jnp.bfloat16)
    facc[...] = jnp.zeros_like(facc)
    pl.semaphore_wait(known.at[2], 7)
    greet(known.at[3])

    up, down, over = c * 4 + lax.rem(y + 1, 4), c * 4 + lax.rem(y + 3, 4), c * 4 + lax.rem(y + 2, 4)
    up_y, down_y, other = (ga, bai(1, 0, c)), (ga, bai(-1, 0, c)), (ga, bai(0, 0, 1 - c))
    sends = []

    def launch(cp):
        cp.start()
        sends.append(cp)

    def to_y(index, view, device):
        return remote(view, view, w2s.at[index], w2r.at[index], device)

    def to_core(index, view):
        return remote(view, view, w3s.at[index], w3r.at[index], other)

    def x_first(h):
        part = pl.ds(3 * h, 3)
        return remote(wd.at[own, part], stage.at[part], xs.at[h], xr.at[h], beyond)

    def x_second(h):
        part = pl.ds(3 * h, 3)
        return remote(
            stage.at[part], wd.at[here * 2 + swap, part], xs.at[2 + h], xr.at[2 + h], (gai(0, 1), ba)
        )

    def fwd(k):
        hop(UP1, k).wait_recv()
        hop(UP2, k).start()
        hop(DN1, k).wait_recv()
        hop(DN2, 2 * k).start()
        hop(DN2, 2 * k + 1).start()

    lane = lax.broadcasted_iota(jnp.int32, (64, 128), 1) // 64

    def accumulate(per_band, first_band):
        for f in range(2):
            total = facc[pl.ds(f * 64, 64), :]
            for q in range(per_band.shape[0] // 64):
                part = per_band[q * 64 : (q + 1) * 64, (q // 2) * 128 : (q // 2 + 1) * 128]
                total += jnp.where(lane == q % 2, part * bf_ref[f, first_band + q], 0.0)
            facc[pl.ds(f * 64, 64), :] = total

    def by_column(applied, right):
        high, low = halves(applied)
        return dot_nt(high, right) + dot_nt(low, right)

    def by_row(left, turned):
        high, low = halves(turned)
        return dot(left, high) + dot(left, low)

    def block(index):
        if index < NEAR:
            return wn[:, index].reshape(GB, GB)
        return wd[:, index - NEAR].reshape(GB, GB)

    def early(e):
        rows = pl.ds(pl.multiple_of(e * 256, 256), 256)
        hop(X0, 2 * e).wait_recv()
        hop(X0, 2 * e + 1).wait_recv()
        a0 = mv[A0, rows, :]
        applied = dot(a0, wown[A0])
        for slot in (A1, AM1, B0):
            applied += dot(mv[slot, rows, :], wown[slot])
        accumulate(by_column(applied, a0), 4 * e)
        t2[:, rows] = dot_nt(wown[A2], a0)
        tm2[:, rows] = dot_nt(wown[AM2], a0)
        tb2[:, rows] = dot_nt(wown[B2], a0)

    def near(e):
        rows = pl.ds(pl.multiple_of(e * 256, 256), 256)
        am1, a1, b0 = mv[AM1, rows, :], mv[A1, rows, :], mv[B0, rows, :]
        accumulate(by_column(dot(am1, block(0)) + dot(a1, block(1)), b0), 4 * e)
        tm2[:, rows] += dot_nt(block(2), b0)

    def middle(e):
        rows = pl.ds(pl.multiple_of(e * 256, 256), 256)
        am1, a1 = mv[AM1, rows, :], mv[A1, rows, :]
        tm2[:, rows] += dot_nt(block(3), a1)
        t2[:, rows] += dot_nt(block(4), am1)
        tb2[:, rows] += dot_nt(block(5), am1)
        ab2[rows, :] = dot(am1, block(8))

    def late(k, count=1):
        rows = pl.ds(k * CH, count * CH)
        for j in range(count):
            hop(UP2, k + j).wait_recv()
        am2 = mv[AM2, rows, :]
        tb2[:, rows] += dot_nt(block(7), am2)
        turned = t2[:, rows] + dot_nt(block(6), am2)
        accumulate(by_row(mv[A2, rows, :], turned) + by_row(am2, tm2[:, rows]), 2 * k)

    def last(k, count=1):
        rows = pl.ds(k * CH, count * CH)
        for j in range(2 * count):
            hop(X2, 2 * k + j).wait_recv()
        b2 = mv[B2, rows, :]
        accumulate(by_row(b2, tb2[:, rows]) + by_column(ab2[rows, :], b2), 2 * k)

    def cross(k):
        for h in range(2):
            hop(DN2, 2 * k + h).wait_recv()
            hop(X2, 2 * k + h).start()

    wait_bytes(wn.at[here], w1r.at[0])
    launch(to_y(0, wn.at[here], up_y))
    launch(to_y(1, wn.at[here], down_y))
    launch(to_core(0, wn.at[here]))
    fwd(0)
    fwd(1)
    wait_bytes(wd.at[own], w1r.at[1])
    launch(x_first(0))
    launch(x_first(1))
    launch(to_y(3, wd.at[own], up_y))
    launch(to_y(4, wd.at[own], down_y))
    launch(to_core(4, wd.at[own]))
    fwd(2)
    hop(X0, 5).start()
    to_y(0, wn.at[down], up_y).wait_recv()
    launch(to_y(2, wn.at[down], up_y))
    launch(to_core(1, wn.at[down]))
    to_y(1, wn.at[up], up_y).wait_recv()
    launch(to_core(2, wn.at[up]))
    fwd(3)
    for h in range(2):
        x_first(h).wait_recv()
        launch(x_second(h))
    fwd(4)
    hop(X0, 6).start()
    hop(X0, 7).start()
    own_f.wait()
    own_m.wait()
    for cp in own_w:
        cp.wait()
    early(0)
    to_y(3, wd.at[down * 2 + same], up_y).wait_recv()
    launch(to_y(7, wd.at[down * 2 + same], up_y))
    launch(to_core(5, wd.at[down * 2 + same]))
    to_y(4, wd.at[up * 2 + same], up_y).wait_recv()
    launch(to_core(6, wd.at[up * 2 + same]))
    fwd(5)
    early(1)
    to_y(2, wn.at[over], up_y).wait_recv()
    launch(to_core(3, wn.at[over]))
    fwd(6)
    mirror = (1 - 2 * c) * 4
    for index, slot in enumerate((here, down, up, over)):
        to_core(index, wn.at[slot + mirror]).wait_recv()
    near(0)
    fwd(7)
    x_second(0).wait_recv()
    x_second(1).wait_recv()
    launch(to_y(5, wd.at[here * 2 + swap], up_y))
    launch(to_y(6, wd.at[here * 2 + swap], down_y))
    launch(to_core(7, wd.at[here * 2 + swap]))
    to_y(7, wd.at[over * 2 + same], up_y).wait_recv()
    launch(to_core(8, wd.at[over * 2 + same]))
    near(1)
    cross(0)
    early(2)
    cross(1)
    to_y(6, wd.at[up * 2 + swap], up_y).wait_recv()
    launch(to_y(8, wd.at[up * 2 + swap], down_y))
    launch(to_core(9, wd.at[up * 2 + swap]))
    to_y(5, wd.at[down * 2 + swap], up_y).wait_recv()
    launch(to_core(10, wd.at[down * 2 + swap]))
    near(2)
    cross(2)
    pl.semaphore_wait(known.at[3], 7)
    early(3)
    cross(3)
    near(3)
    to_y(8, wd.at[over * 2 + swap], up_y).wait_recv()
    launch(to_core(11, wd.at[over * 2 + swap]))
    cross(4)
    for index, slot in enumerate((
        here * 2 + same, down * 2 + same, up * 2 + same, here * 2 + swap,
        over * 2 + same, up * 2 + swap, down * 2 + swap, over * 2 + swap,
    )):
        to_core(4 + index, wd.at[slot + 2 * mirror]).wait_recv()

    middle(0)
    middle(1)
    cross(5)
    middle(2)
    late(0, 2)
    last(0, 2)
    cross(6)
    late(2, 2)
    middle(3)
    late(4, 2)
    cross(7)
    last(2, 2)
    late(6)
    last(4, 2)
    last(6)
    late(7)
    last(7)

    full = facc[...]
    x1 = full.astype(jnp.bfloat16)
    rest = full - x1.astype(jnp.float32)
    x2 = rest.astype(jnp.bfloat16)
    picked = dot(x1, one_n[...]) + dot(x2, one_n[...])
    one_m = lax.broadcasted_iota(jnp.int32, (64, 2048), 0) == pp[0:1, :]
    for f in range(2):
        row = jnp.sum(jnp.where(one_m, picked[f * 64 : (f + 1) * 64], 0.0), axis=0, keepdims=True)
        for a in range(16):
            red_src[a, f : f + 1, :] = row[:, a * 128 : (a + 1) * 128]

    for k in FAR_FIRST:
        peer = lax.rem(ga + k, 16)
        remote(red_src.at[peer], red_a.at[k - 1], r1s, r1r, (peer, ba)).start()

    wait_bytes(wn.at[here], w1s.at[0])
    wait_bytes(wd.at[own], w1s.at[1])
    for cp in sends:
        cp.wait_send()

    @pl.loop(0, NCH)
    def _(k):
        for flow in (UP1, DN1, UP2, X0):
            hop(flow, k).wait_send()
        for flow in (DN2, X2):
            hop(flow, 2 * k).wait_send()
            hop(flow, 2 * k + 1).wait_send()

    wait_bytes(red_a, r1r)
    mine = red_src[ga]
    for k in range(15):
        mine += red_a[k]
    red_b[...] = mine
    keep = pltpu.make_async_copy(red_b, out_ref.at[ba], ploc)
    keep.start()

    for k in FAR_FIRST:
        peer = lax.rem(ba + k, 16)
        remote(red_b, out_ref.at[ba], r2s, r2r, (ga, peer)).start()

    wait_bytes(red_a, r1s)
    keep.wait()
    wait_bytes(red_a, r2s)
    wait_bytes(out_ref.at[pl.ds(0, 15)], r2r)


def shards(matrix_elements, screening, band_factor, pair_list):
    bands, quasi, width = matrix_elements.shape
    dma = pltpu.SemaphoreType.DMA
    parts = pl.pallas_call(
        kernel,
        out_shape=jax.ShapeDtypeStruct((16, 2, 128), jnp.float32),
        in_specs=[
            pl.BlockSpec(memory_space=pltpu.HBM),
            pl.BlockSpec(memory_space=pltpu.HBM),
            pl.BlockSpec(memory_space=pltpu.HBM),
            pl.BlockSpec(memory_space=pltpu.HBM),
        ],
        out_specs=pl.BlockSpec(memory_space=pltpu.HBM),
        scratch_shapes=[
            pltpu.VMEM((7, 1024, GB), jnp.bfloat16),
            pltpu.VMEM((7, GB, GB), jnp.bfloat16),
            pltpu.VMEM((8, NEAR, 64, GB), jnp.bfloat16),
            pltpu.VMEM((16, FAR, 32, GB), jnp.bfloat16),
            pltpu.VMEM((FAR, 32, GB), jnp.bfloat16),
            pltpu.VMEM((GB, 1024), jnp.float32),
            pltpu.VMEM((GB, 1024), jnp.float32),
            pltpu.VMEM((GB, 1024), jnp.float32),
            pltpu.VMEM((1024, GB), jnp.float32),
            pltpu.SMEM((2, 16), jnp.float32),
            pltpu.VMEM((2, 2016), jnp.int32),
            pltpu.VMEM((2, 2048), jnp.int32),
            pltpu.VMEM((128, 2048), jnp.bfloat16),
            pltpu.VMEM((128, 128), jnp.float32),
            pltpu.VMEM((16, 2, 128), jnp.float32),
            pltpu.VMEM((15, 2, 128), jnp.float32),
            pltpu.VMEM((2, 128), jnp.float32),
            dma((6, 2 * NCH)), dma((6, 2 * NCH)), dma, dma((7,)), dma, dma,
            pltpu.SemaphoreType.REGULAR((4,)), dma((2,)), dma((2,)), dma((4,)), dma((4,)), dma((9,)), dma((9,)), dma((12,)), dma((12,)),
            dma, dma, dma, dma,
        ],
        compiler_params=pltpu.CompilerParams(
            collective_id=0, has_side_effects=True, vmem_limit_bytes=56 << 20
        ),
        cost_estimate=pl.CostEstimate(flops=9 * 10**9, bytes_accessed=20 << 20, transcendentals=0),
        name="self_energy",
    )(matrix_elements.reshape(bands * quasi, width), screening, band_factor, pair_list)
    return jnp.sum(parts, axis=0)[:, :126]


def solution(mesh):
    placed = (P("ba", None, "ga"), P(None, "ga"), P(None, "ba"), P())
    return jax.shard_map(
        shards, mesh=mesh, in_specs=placed, out_specs=P(None, "ga"), check_vma=False
    )
```

```python
import functools

import jax
import jax.numpy as jnp
from jax import lax
from jax.experimental import pallas as pl
from jax.experimental.pallas import tpu as pltpu
from jax.sharding import PartitionSpec as P

MESH = pl.DeviceIdType.MESH
GB = 512
CH = 128
NCH = 8
NEAR = 3
FAR = 6
A0, A1, AM1, A2, AM2, B0, B2 = range(7)
UP1, UP2, DN1, DN2, X0, X2 = range(6)
FAR_FIRST = (8, 9, 7, 10, 6, 11, 5, 12, 4, 13, 3, 14, 2, 15, 1)
NT = (((1,), (1,)), ((), ()))


def remote(src, dst, send, recv, device):
    return pltpu.make_async_remote_copy(
        src_ref=src, dst_ref=dst, send_sem=send, recv_sem=recv, device_id=device, device_id_type=MESH
    )


def wait_bytes(ref, sem):
    pltpu.make_async_copy(ref, ref, sem).wait()


def dot(a, b):
    return jnp.dot(a, b, preferred_element_type=jnp.float32)


def dot_nt(a, b):
    return lax.dot_general(a, b, NT, preferred_element_type=jnp.float32)


def halves(x):
    high = x.astype(jnp.bfloat16)
    return high, (x - high.astype(jnp.float32)).astype(jnp.bfloat16)


def kernel(
    m_ref, w_ref, factor_ref, pair_ref, out_ref,
    mv, wown, wn, wd, stage, t2, tm2, tb2, ab2, bf_ref, pairs, pp, one_n, facc, red_src, red_a, red_b,
    msend, mrecv, mloc, wloc, ploc, floc, known, w1s, w1r, xs, xr, w2s, w2r, w3s, w3r, r1s, r1r, r2s, r2r,
):
    ga, ba = lax.axis_index("ga"), lax.axis_index("ba")
    z, s = ga // 2, lax.rem(ga, 2)
    y, xh, c = ba // 4, lax.rem(ba // 2, 2), lax.rem(ba, 2)

    def gai(dz, flip=0):
        side = 1 - s if flip else s
        return lax.rem(z + 8 + dz, 8) * 2 + side

    def bai(dy, dx, core):
        return (lax.rem(y + 4 + dy, 4) * 2 + lax.rem(xh + dx, 2)) * 2 + core

    barrier = pltpu.get_barrier_semaphore()

    neighbours = (
        (gai(1), ba), (gai(-1), ba), (gai(0, 1), ba), (gai(0, 1), bai(0, 1, c)),
        (ga, bai(1, 0, c)), (ga, bai(-1, 0, c)), (ga, bai(0, 0, 1 - c)),
    )

    def greet(sem):
        for device in neighbours:
            pl.semaphore_signal(sem, inc=1, device_id=device, device_id_type=MESH)

    greet(barrier)
    own_m = pltpu.make_async_copy(m_ref, mv.at[A0], mloc)
    own_m.start()

    def hop(flow, k):
        size = CH // 2 if flow in (DN2, X2) else CH
        rows = pl.ds(pl.multiple_of(k * size, size), size)
        own_block = m_ref if isinstance(k, int) and k == 0 else mv.at[A0]
        src, dst, target = {
            UP1: (own_block, AM1, gai(1)),
            DN1: (own_block, A1, gai(-1)),
            UP2: (mv.at[AM1], AM2, gai(1)),
            DN2: (mv.at[A1], A2, gai(-1)),
            X0: (own_block, B0, gai(0, 1)),
            X2: (mv.at[A2], B2, gai(0, 1)),
        }[flow]
        return remote(
            src.at[rows], mv.at[dst, rows], msend.at[flow, k], mrecv.at[flow, k], (target, ba)
        )

    def first(k):
        hop(UP1, k).start()
        hop(DN1, k).start()
        if k < 5:
            hop(X0, k).start()

    here = c * 4 + y
    same, swap = xh, 1 - xh
    beyond = (gai(0, 1), bai(0, 1, c))

    def give_near(block, index):
        remote(
            w_ref.at[pl.ds(block * GB + here * 64, 64)], wn.at[here, index], w1s.at[0], w1r.at[0], beyond
        ).start()

    def give_far(device, piece, block, index):
        remote(
            w_ref.at[pl.ds(block * GB + piece * 32, 32)], wd.at[piece, index], w1s.at[1], w1r.at[1], device
        ).start()

    pl.semaphore_wait(barrier, 7)
    first(0)
    greet(known.at[0])
    own = here * 2 + same
    give_near(gai(-1, 1), 0)
    give_near(gai(1, 1), 1)
    give_near(gai(-2, 1), 2)
    give_far((gai(-1), ba), own, gai(-3), 0)
    give_far((gai(1), ba), own, gai(3), 1)
    give_far((gai(1), ba), own, gai(3, 1), 2)
    pl.semaphore_wait(known.at[0], 7)
    greet(known.at[1])
    give_far((gai(2), ba), own, gai(4), 3)
    give_far((gai(2), ba), own, gai(4, 1), 4)
    own_m.wait()
    first(1)
    pl.semaphore_wait(known.at[1], 7)
    greet(known.at[2])
    give_far((gai(-2, 1), bai(0, 1, c)), here * 2 + swap, gai(-3, 1), 5)
    for k in range(2, NCH):
        first(k)

    own_p = pltpu.make_async_copy(pair_ref, pairs, ploc)
    own_p.start()
    own_rows = (
        (A0, gai(0)), (A1, gai(1)), (AM1, gai(-1)), (A2, gai(2)), (AM2, gai(-2)),
        (B0, gai(0, 1)), (B2, gai(2, 1)),
    )
    own_w = []
    for slot, block in own_rows:
        cp = pltpu.make_async_copy(w_ref.at[pl.ds(block * GB, GB)], wown.at[slot], wloc.at[slot])
        cp.start()
        own_w.append(cp)
    own_f = pltpu.make_async_copy(factor_ref, bf_ref, floc)
    own_f.start()

    own_p.wait()
    pp[...] = jnp.full(pp.shape, -1, jnp.int32)
    for a in range(16):
        pp[:, a * 128 : a * 128 + 126] = pairs[:, a * 126 : (a + 1) * 126]
    band = lax.rem(lax.broadcasted_iota(jnp.int32, (128, 2048), 0), 64)
    one_n[...] = jnp.where(band == pp[1:2, :], 1.0, 0.0).astype(jnp.bfloat16)
    facc[...] = jnp.zeros_like(facc)
    pl.semaphore_wait(known.at[2], 7)
    greet(known.at[3])

    up, down, over = c * 4 + lax.rem(y + 1, 4), c * 4 + lax.rem(y + 3, 4), c * 4 + lax.rem(y + 2, 4)
    up_y, down_y, other = (ga, bai(1, 0, c)), (ga, bai(-1, 0, c)), (ga, bai(0, 0, 1 - c))
    sends = []

    def launch(cp):
        cp.start()
        sends.append(cp)

    def to_y(index, view, device):
        return remote(view, view, w2s.at[index], w2r.at[index], device)

    def to_core(index, view):
        return remote(view, view, w3s.at[index], w3r.at[index], other)

    def x_first(h):
        part = pl.ds(3 * h, 3)
        return remote(wd.at[own, part], stage.at[part], xs.at[h], xr.at[h], beyond)

    def x_second(h):
        part = pl.ds(3 * h, 3)
        return remote(
            stage.at[part], wd.at[here * 2 + swap, part], xs.at[2 + h], xr.at[2 + h], (gai(0, 1), ba)
        )

    def fwd(k):
        hop(UP1, k).wait_recv()
        hop(UP2, k).start()
        hop(DN1, k).wait_recv()
        hop(DN2, 2 * k).start()
        hop(DN2, 2 * k + 1).start()

    lane = lax.broadcasted_iota(jnp.int32, (64, 128), 1) // 64

    def accumulate(per_band, first_band):
        for f in range(2):
            total = facc[pl.ds(f * 64, 64), :]
            for q in range(per_band.shape[0] // 64):
                part = per_band[q * 64 : (q + 1) * 64, (q // 2) * 128 : (q // 2 + 1) * 128]
                total += jnp.where(lane == q % 2, part * bf_ref[f, first_band + q], 0.0)
            facc[pl.ds(f * 64, 64), :] = total

    def by_column(applied, right):
        high, low = halves(applied)
        return dot_nt(high, right) + dot_nt(low, right)

    def by_row(left, turned):
        high, low = halves(turned)
        return dot(left, high) + dot(left, low)

    def block(index):
        if index < NEAR:
            return wn[:, index].reshape(GB, GB)
        return wd[:, index - NEAR].reshape(GB, GB)

    def early(e):
        rows = pl.ds(pl.multiple_of(e * 256, 256), 256)
        hop(X0, 2 * e).wait_recv()
        hop(X0, 2 * e + 1).wait_recv()
        a0 = mv[A0, rows, :]
        applied = dot(a0, wown[A0])
        for slot in (A1, AM1, B0):
            applied += dot(mv[slot, rows, :], wown[slot])
        accumulate(by_column(applied, a0), 4 * e)
        t2[:, rows] = dot_nt(wown[A2], a0)
        tm2[:, rows] = dot_nt(wown[AM2], a0)
        tb2[:, rows] = dot_nt(wown[B2], a0)

    def near(e):
        rows = pl.ds(pl.multiple_of(e * 256, 256), 256)
        am1, a1, b0 = mv[AM1, rows, :], mv[A1, rows, :], mv[B0, rows, :]
        accumulate(by_column(dot(am1, block(0)) + dot(a1, block(1)), b0), 4 * e)
        tm2[:, rows] += dot_nt(block(2), b0)

    def middle(e):
        rows = pl.ds(pl.multiple_of(e * 256, 256), 256)
        am1, a1 = mv[AM1, rows, :], mv[A1, rows, :]
        tm2[:, rows] += dot_nt(block(3), a1)
        t2[:, rows] += dot_nt(block(4), am1)
        tb2[:, rows] += dot_nt(block(5), am1)
        ab2[rows, :] = dot(am1, block(8))

    def late(k, count=1):
        rows = pl.ds(k * CH, count * CH)
        for j in range(count):
            hop(UP2, k + j).wait_recv()
        am2 = mv[AM2, rows, :]
        tb2[:, rows] += dot_nt(block(7), am2)
        turned = t2[:, rows] + dot_nt(block(6), am2)
        accumulate(by_row(mv[A2, rows, :], turned) + by_row(am2, tm2[:, rows]), 2 * k)

    def last(k, count=1):
        rows = pl.ds(k * CH, count * CH)
        for j in range(2 * count):
            hop(X2, 2 * k + j).wait_recv()
        b2 = mv[B2, rows, :]
        accumulate(by_row(b2, tb2[:, rows]) + by_column(ab2[rows, :], b2), 2 * k)

    def cross(k):
        for h in range(2):
            hop(DN2, 2 * k + h).wait_recv()
            hop(X2, 2 * k + h).start()

    wait_bytes(wn.at[here], w1r.at[0])
    launch(to_y(0, wn.at[here], up_y))
    launch(to_y(1, wn.at[here], down_y))
    launch(to_core(0, wn.at[here]))
    fwd(0)
    fwd(1)
    wait_bytes(wd.at[own], w1r.at[1])
    launch(x_first(0))
    launch(x_first(1))
    launch(to_y(3, wd.at[own], up_y))
    launch(to_y(4, wd.at[own], down_y))
    launch(to_core(4, wd.at[own]))
    fwd(2)
    hop(X0, 5).start()
    to_y(0, wn.at[down], up_y).wait_recv()
    launch(to_y(2, wn.at[down], up_y))
    launch(to_core(1, wn.at[down]))
    to_y(1, wn.at[up], up_y).wait_recv()
    launch(to_core(2, wn.at[up]))
    fwd(3)
    for h in range(2):
        x_first(h).wait_recv()
        launch(x_second(h))
    fwd(4)
    hop(X0, 6).start()
    hop(X0, 7).start()
    own_f.wait()
    for cp in own_w:
        cp.wait()
    early(0)
    to_y(3, wd.at[down * 2 + same], up_y).wait_recv()
    launch(to_y(7, wd.at[down * 2 + same], up_y))
    launch(to_core(5, wd.at[down * 2 + same]))
    to_y(4, wd.at[up * 2 + same], up_y).wait_recv()
    launch(to_core(6, wd.at[up * 2 + same]))
    fwd(5)
    early(1)
    to_y(2, wn.at[over], up_y).wait_recv()
    launch(to_core(3, wn.at[over]))
    fwd(6)
    mirror = (1 - 2 * c) * 4
    for index, slot in enumerate((here, down, up, over)):
        to_core(index, wn.at[slot + mirror]).wait_recv()
    near(0)
    fwd(7)
    x_second(0).wait_recv()
    x_second(1).wait_recv()
    launch(to_y(5, wd.at[here * 2 + swap], up_y))
    launch(to_y(6, wd.at[here * 2 + swap], down_y))
    launch(to_core(7, wd.at[here * 2 + swap]))
    to_y(7, wd.at[over * 2 + same], up_y).wait_recv()
    launch(to_core(8, wd.at[over * 2 + same]))
    near(1)
    cross(0)
    early(2)
    cross(1)
    to_y(6, wd.at[up * 2 + swap], up_y).wait_recv()
    launch(to_y(8, wd.at[up * 2 + swap], down_y))
    launch(to_core(9, wd.at[up * 2 + swap]))
    to_y(5, wd.at[down * 2 + swap], up_y).wait_recv()
    launch(to_core(10, wd.at[down * 2 + swap]))
    near(2)
    cross(2)
    pl.semaphore_wait(known.at[3], 7)
    early(3)
    cross(3)
    near(3)
    to_y(8, wd.at[over * 2 + swap], up_y).wait_recv()
    launch(to_core(11, wd.at[over * 2 + swap]))
    cross(4)
    for index, slot in enumerate((
        here * 2 + same, down * 2 + same, up * 2 + same, here * 2 + swap,
        over * 2 + same, up * 2 + swap, down * 2 + swap, over * 2 + swap,
    )):
        to_core(4 + index, wd.at[slot + 2 * mirror]).wait_recv()

    middle(0)
    middle(1)
    cross(5)
    middle(2)
    late(0, 2)
    last(0, 2)
    cross(6)
    late(2, 2)
    middle(3)
    late(4, 2)
    cross(7)
    last(2, 2)
    late(6)
    last(4, 2)
    last(6)
    late(7)
    last(7)

    full = facc[...]
    x1 = full.astype(jnp.bfloat16)
    rest = full - x1.astype(jnp.float32)
    x2 = rest.astype(jnp.bfloat16)
    picked = dot(x1, one_n[...]) + dot(x2, one_n[...])
    one_m = lax.broadcasted_iota(jnp.int32, (64, 2048), 0) == pp[0:1, :]
    for f in range(2):
        row = jnp.sum(jnp.where(one_m, picked[f * 64 : (f + 1) * 64], 0.0), axis=0, keepdims=True)
        for a in range(16):
            red_src[a, f : f + 1, :] = row[:, a * 128 : (a + 1) * 128]

    for k in FAR_FIRST:
        peer = lax.rem(ga + k, 16)
        remote(red_src.at[peer], red_a.at[k - 1], r1s, r1r, (peer, ba)).start()

    wait_bytes(wn.at[here], w1s.at[0])
    wait_bytes(wd.at[own], w1s.at[1])
    for cp in sends:
        cp.wait_send()

    @pl.loop(0, NCH)
    def _(k):
        for flow in (UP1, DN1, UP2, X0):
            hop(flow, k).wait_send()
        for flow in (DN2, X2):
            hop(flow, 2 * k).wait_send()
            hop(flow, 2 * k + 1).wait_send()

    wait_bytes(red_a, r1r)
    mine = red_src[ga]
    for k in range(15):
        mine += red_a[k]
    red_b[...] = mine
    keep = pltpu.make_async_copy(red_b, out_ref.at[ba], ploc)
    keep.start()

    for k in FAR_FIRST:
        peer = lax.rem(ba + k, 16)
        remote(red_b, out_ref.at[ba], r2s, r2r, (ga, peer)).start()

    wait_bytes(red_a, r1s)
    keep.wait()
    wait_bytes(red_a, r2s)
    wait_bytes(out_ref.at[pl.ds(0, 15)], r2r)


def shards(matrix_elements, screening, band_factor, pair_list):
    bands, quasi, width = matrix_elements.shape
    dma = pltpu.SemaphoreType.DMA
    parts = pl.pallas_call(
        kernel,
        out_shape=jax.ShapeDtypeStruct((16, 2, 128), jnp.float32),
        in_specs=[
            pl.BlockSpec(memory_space=pltpu.HBM),
            pl.BlockSpec(memory_space=pltpu.HBM),
            pl.BlockSpec(memory_space=pltpu.HBM),
            pl.BlockSpec(memory_space=pltpu.HBM),
        ],
        out_specs=pl.BlockSpec(memory_space=pltpu.HBM),
        scratch_shapes=[
            pltpu.VMEM((7, 1024, GB), jnp.bfloat16),
            pltpu.VMEM((7, GB, GB), jnp.bfloat16),
            pltpu.VMEM((8, NEAR, 64, GB), jnp.bfloat16),
            pltpu.VMEM((16, FAR, 32, GB), jnp.bfloat16),
            pltpu.VMEM((FAR, 32, GB), jnp.bfloat16),
            pltpu.VMEM((GB, 1024), jnp.float32),
            pltpu.VMEM((GB, 1024), jnp.float32),
            pltpu.VMEM((GB, 1024), jnp.float32),
            pltpu.VMEM((1024, GB), jnp.float32),
            pltpu.SMEM((2, 16), jnp.float32),
            pltpu.VMEM((2, 2016), jnp.int32),
            pltpu.VMEM((2, 2048), jnp.int32),
            pltpu.VMEM((128, 2048), jnp.bfloat16),
            pltpu.VMEM((128, 128), jnp.float32),
            pltpu.VMEM((16, 2, 128), jnp.float32),
            pltpu.VMEM((15, 2, 128), jnp.float32),
            pltpu.VMEM((2, 128), jnp.float32),
            dma((6, 2 * NCH)), dma((6, 2 * NCH)), dma, dma((7,)), dma, dma,
            pltpu.SemaphoreType.REGULAR((4,)), dma((2,)), dma((2,)), dma((4,)), dma((4,)), dma((9,)), dma((9,)), dma((12,)), dma((12,)),
            dma, dma, dma, dma,
        ],
        compiler_params=pltpu.CompilerParams(
            collective_id=0, has_side_effects=True, vmem_limit_bytes=56 << 20
        ),
        cost_estimate=pl.CostEstimate(flops=9 * 10**9, bytes_accessed=20 << 20, transcendentals=0),
        name="self_energy",
    )(matrix_elements.reshape(bands * quasi, width), screening, band_factor, pair_list)
    return jnp.sum(parts, axis=0)[:, :126]


def solution(mesh):
    placed = (P("ba", None, "ga"), P(None, "ga"), P(None, "ba"), P())
    return jax.shard_map(
        shards, mesh=mesh, in_specs=placed, out_specs=P(None, "ga"), check_vma=False
    )
```
